128 devices in a mesh: band: 16 (over z, x), patch: 8 (over y, core).
Axes of the slice: x: 4, y: 4, z: 4, core: 2. Of those that a mesh axis runs over, the one named last changes fastest.
Arguments:
- grid_latent: bfloat16 [32768, 512], P(('band', 'patch')), may hold values from -6 to 6
- mesh_latent: bfloat16 [16384, 512], P(('band', 'patch')), may hold values from -6 to 6
- grid_cotangent: bfloat16 [32768, 512], P(('band', 'patch')), may hold values from -6 to 6
- enc_w_send: bfloat16 [512, 512], replicated, may hold values from -0.25 to 0.25
- enc_w_recv: bfloat16 [512, 512], replicated, may hold values from -0.25 to 0.25
- enc_w_out: bfloat16 [512, 512], replicated, may hold values from -0.25 to 0.25
- dec_w_send: bfloat16 [512, 512], replicated, may hold values from -0.25 to 0.25
- dec_w_recv: bfloat16 [512, 512], replicated, may hold values from -0.25 to 0.25
- dec_w_out: bfloat16 [512, 512], replicated, may hold values from -0.25 to 0.25
- enc_sender: int32 [128, 3, 8, 32], P(('band', 'patch')), may hold values from 0 to 255
- enc_receiver: int32 [128, 3, 8, 32], P(('band', 'patch')), may hold values from 0 to 127
- enc_count: int32 [128, 3, 8], P(('band', 'patch')), may hold values from 0 to 32, as said below
- dec_sender: int32 [128, 3, 8, 32], P(('band', 'patch')), may hold values from 0 to 127
- dec_receiver: int32 [128, 3, 8, 32], P(('band', 'patch')), may hold values from 0 to 255
- dec_count: int32 [128, 3, 8], P(('band', 'patch')), may hold values from 0 to 32, as said below
Outputs:
- grid_grad: float32 [32768, 512], P(('band', 'patch'))
- mesh_grad: float32 [16384, 512], P(('band', 'patch'))
- grad_enc_send: float32 [512, 512], replicated
- grad_enc_recv: float32 [512, 512], replicated
- grad_enc_out: float32 [512, 512], replicated
- grad_dec_send: float32 [512, 512], replicated
- grad_dec_recv: float32 [512, 512], replicated
- grad_dec_out: float32 [512, 512], replicated
The draws below stay inside these ranges and needn't reach their ends.
Inputs may be any that keep to these rules, and one draw needn't show every extreme that they name: enc_count[m, o, p] is 0 exactly where the source band b - o + 1 lies outside the bands, and at least 1 elsewhere; one mesh device holds 32 live slots from every source device that it has. dec_count[d, o, q] is 0 exactly where the source band b - o + 1 lies outside the bands, and at least 1 elsewhere; one grid device holds 32 live slots from every source device that it has.
All inputs are finite; a program needn't handle non-finite values.
Results may differ from the reference program's by a relative error of at most 0.0095.
Values may be sent and summed in bfloat16 or wider, within the bound.
A program may use at most 64 MiB of HBM per device.

```python
import jax
import jax.numpy as jnp

L = 512
GD = 256
MD = 128
CAP = 32
GRID = 32768
MESH = 16384
N_BAND = 16
N_PATCH = 8
DEVICES = 128


def band_counts(key):
    devices = N_BAND * N_PATCH
    base = jax.random.randint(jax.random.fold_in(key, 1), (devices, 3, N_PATCH), 0, CAP, dtype=jnp.int32)
    chosen = jax.random.randint(jax.random.fold_in(key, 2), (), 0, devices, dtype=jnp.int32)
    owner = jnp.arange(devices, dtype=jnp.int32)
    band_of = owner // N_PATCH
    margin = max(N_BAND // 4, 1)
    factor = jnp.where((band_of < margin) | (band_of >= N_BAND - margin), 4, 2)[:, None, None]
    counted = jnp.minimum(CAP, 1 + CAP // 4 + base * factor // 4)
    counted = jnp.where(owner[:, None, None] == chosen, CAP, counted)
    source_band = band_of[:, None] - jnp.arange(3, dtype=jnp.int32)[None, :] + 1
    inside = (source_band >= 0) & (source_band < N_BAND)
    counted = jnp.where(inside[:, :, None], counted, 0)
    return counted.astype(jnp.int32)


def draw_enc_count(key, part):
    key = jax.random.fold_in(key, 11)
    return band_counts(key)


def draw_dec_count(key, part):
    key = jax.random.fold_in(key, 12)
    return band_counts(key)


def with_ends(result, stream_key, low, largest):
    longest = result.shape.index(max(result.shape))
    spots = []
    for shift in (0, 1):
        where = [jax.random.randint(jax.random.fold_in(stream_key, axis), (), 0, length) for axis, length in enumerate(result.shape)]
        where[longest] = (where[longest] + shift) % result.shape[longest]
        spots.append(tuple(where))
    return result.at[spots[0]].set(low).at[spots[1]].set(largest)


def block_levels(stream_key, extent, split, low, top_value):
    level, own = 1.0, jax.random.fold_in(stream_key, 6)
    for position, parts in split:
        draws = jnp.exp(jax.random.uniform(jax.random.fold_in(own, position), (parts,), jnp.float32, low / len(split), top_value / len(split)))
        level = level * jnp.repeat(draws, extent[position] // parts).reshape([-1 if axis == position else 1 for axis in range(len(extent))])
    return level


def centred(stream_key, extent, deviation, limit, cuts=(), kind=jnp.bfloat16):
    drawn = deviation * jax.random.normal(stream_key, extent, jnp.float32)
    if cuts:
        drawn = drawn * block_levels(stream_key, extent, cuts, -0.22, 0.18)
    return jnp.clip(drawn, -limit, limit).astype(kind)


def setup_inputs(seed: int = 0) -> dict:
    streams_of = jax.random.split(jax.random.key(seed), 16)
    return {
        "grid_latent": centred(streams_of[0], (GRID, L), 1.0, 6.0, ((0, 128),)),
        "mesh_latent": centred(streams_of[1], (MESH, L), 1.0, 6.0, ((0, 128),)),
        "grid_cotangent": centred(streams_of[2], (GRID, L), 1.0, 6.0, ((0, 128),)),
        "enc_w_send": centred(streams_of[3], (L, L), L ** -0.5, 0.25),
        "enc_w_recv": centred(streams_of[4], (L, L), L ** -0.5, 0.25),
        "enc_w_out": centred(streams_of[5], (L, L), L ** -0.5, 0.25),
        "dec_w_send": centred(streams_of[6], (L, L), L ** -0.5, 0.25),
        "dec_w_recv": centred(streams_of[7], (L, L), L ** -0.5, 0.25),
        "dec_w_out": centred(streams_of[8], (L, L), L ** -0.5, 0.25),
        "enc_sender": with_ends(jax.random.randint(streams_of[9], (DEVICES, 3, N_PATCH, CAP), 0, GD), jax.random.fold_in(streams_of[9], 1), 0, GD - 1).astype(jnp.int32),
        "enc_receiver": with_ends(jax.random.randint(streams_of[10], (DEVICES, 3, N_PATCH, CAP), 0, MD), jax.random.fold_in(streams_of[10], 1), 0, MD - 1).astype(jnp.int32),
        "enc_count": draw_enc_count(jax.random.fold_in(streams_of[15], 71), 0),
        "dec_sender": with_ends(jax.random.randint(streams_of[12], (DEVICES, 3, N_PATCH, CAP), 0, MD), jax.random.fold_in(streams_of[12], 1), 0, MD - 1).astype(jnp.int32),
        "dec_receiver": with_ends(jax.random.randint(streams_of[13], (DEVICES, 3, N_PATCH, CAP), 0, GD), jax.random.fold_in(streams_of[13], 1), 0, GD - 1).astype(jnp.int32),
        "dec_count": draw_dec_count(jax.random.fold_in(streams_of[15], 71), 0),
    }


def product(left, right):
    return jnp.dot(left, right, preferred_element_type=jnp.float32)


def silu_slope(value):
    sigma = jax.nn.sigmoid(value)
    return sigma * (1.0 + value * (1.0 - sigma))


def slot_lists(sender, receiver, count, send_rows, recv_rows):
    devices = N_BAND * N_PATCH
    target = jnp.arange(devices, dtype=jnp.int32)[:, None, None, None]
    offset = jnp.arange(3, dtype=jnp.int32)[None, :, None, None]
    column = jnp.arange(N_PATCH, dtype=jnp.int32)[None, None, :, None]
    slot_ids = jnp.arange(CAP, dtype=jnp.int32)[None, None, None, :]
    target_band = target // N_PATCH
    target_patch = target % N_PATCH
    source_band = jnp.clip(target_band - offset + 1, 0, N_BAND - 1)
    source = (source_band * N_PATCH + column).astype(jnp.int32)
    picked = sender[source, offset, target_patch, slot_ids]
    src = (source * send_rows + picked).reshape(-1).astype(jnp.int32)
    dst = (target * recv_rows + receiver).reshape(-1).astype(jnp.int32)
    live = (slot_ids < count[:, :, :, None]).reshape(-1)[:, None]
    return src, dst, live


def reference(grid_latent, mesh_latent, grid_cotangent, enc_w_send, enc_w_recv, enc_w_out, dec_w_send, dec_w_recv, dec_w_out, enc_sender, enc_receiver, enc_count, dec_sender, dec_receiver, dec_count):
    devices = N_BAND * N_PATCH
    grid_nodes = grid_latent.shape[0]
    mesh_nodes = mesh_latent.shape[0]
    enc_src, enc_dst, enc_live = slot_lists(enc_sender, enc_receiver, enc_count, GD, MD)
    dec_src, dec_dst, dec_live = slot_lists(dec_sender, dec_receiver, dec_count, MD, GD)

    sender_rows = grid_latent[enc_src]
    receiver_rows = mesh_latent[enc_dst]
    enc_pre = product(sender_rows, enc_w_send) + product(receiver_rows, enc_w_recv)
    enc_act = jax.nn.silu(enc_pre).astype(jnp.bfloat16)
    enc_msg = jnp.where(enc_live, product(enc_act, enc_w_out), jnp.float32(0.0))
    mesh_new = (mesh_latent.astype(jnp.float32) + jax.ops.segment_sum(enc_msg, enc_dst, mesh_nodes)).astype(jnp.bfloat16)

    mesh_rows = mesh_new[dec_src]
    grid_rows = grid_latent[dec_dst]
    dec_pre = product(mesh_rows, dec_w_send) + product(grid_rows, dec_w_recv)
    dec_act = jax.nn.silu(dec_pre).astype(jnp.bfloat16)
    dec_gmsg = jnp.where(dec_live, grid_cotangent[dec_dst], jnp.zeros((), jnp.bfloat16)).astype(jnp.bfloat16)
    dec_dpre = (product(dec_gmsg, dec_w_out.T) * silu_slope(dec_pre)).astype(jnp.bfloat16)
    dec_dsend = product(dec_dpre, dec_w_send.T).astype(jnp.bfloat16)
    mesh_grad_new = jax.ops.segment_sum(dec_dsend.astype(jnp.float32), dec_src, mesh_nodes)

    enc_gmsg = jnp.where(enc_live, mesh_grad_new.astype(jnp.bfloat16)[enc_dst], jnp.zeros((), jnp.bfloat16)).astype(jnp.bfloat16)
    enc_dpre = (product(enc_gmsg, enc_w_out.T) * silu_slope(enc_pre)).astype(jnp.bfloat16)
    enc_dsend = product(enc_dpre, enc_w_send.T).astype(jnp.bfloat16)

    grid_grad = grid_cotangent.astype(jnp.float32) + jax.ops.segment_sum(product(dec_dpre, dec_w_recv.T), dec_dst, grid_nodes)
    grid_grad = grid_grad + jax.ops.segment_sum(enc_dsend.astype(jnp.float32), enc_src, grid_nodes)
    mesh_grad = mesh_grad_new + jax.ops.segment_sum(product(enc_dpre, enc_w_recv.T), enc_dst, mesh_nodes)

    factor = float(devices * 3 * N_PATCH * CAP) ** -0.5
    grad_enc_send = product(sender_rows.T, enc_dpre) * factor
    grad_enc_recv = product(receiver_rows.T, enc_dpre) * factor
    grad_enc_out = product(enc_act.T, enc_gmsg) * factor
    grad_dec_send = product(mesh_rows.T, dec_dpre) * factor
    grad_dec_recv = product(grid_rows.T, dec_dpre) * factor
    grad_dec_out = product(dec_act.T, dec_gmsg) * factor
    return (grid_grad, mesh_grad, grad_enc_send, grad_enc_recv, grad_enc_out, grad_dec_send, grad_dec_recv, grad_dec_out)
```

```python
import functools
import itertools

import jax
import jax.numpy as jnp
from jax import lax
from jax.experimental import pallas as pl
from jax.experimental.pallas import tpu as pltpu
from jax.sharding import PartitionSpec as P

MESH = pl.DeviceIdType.MESH
NB, NP = 16, 8
SIZES = {"z": 4, "x": 4, "y": 4, "c": 2}

def position():
    b, p = lax.axis_index("band"), lax.axis_index("patch")
    return {"z": b // 4, "x": lax.rem(b, 4), "y": p // 2, "c": lax.rem(p, 2)}

def device(pos):
    return (pos["z"] * 4 + pos["x"], pos["y"] * 2 + pos["c"])

def offsets(axes):
    return [d for d in itertools.product(*[range(SIZES[a]) for a in axes]) if any(d)]

def partner(pos, axes, d):
    new = dict(pos)
    for a, k in zip(axes, d):
        new[a] = lax.rem(pos[a] + k, SIZES[a])
    return new

def index(pos, axes):
    i = 0
    for a in axes:
        i = i * SIZES[a] + pos[a]
    return i

def geometry(plan):
    R = C = 512
    out = []
    for axes in plan:
        g = 1
        for a in axes:
            g *= SIZES[a]
        rs = min(g, R // 16)
        cs = g // rs
        out.append((axes, g, (R, C), (R // rs, C // cs), cs))
        R, C = R // rs, C // cs
    return out

def scratch_for(plan):
    shapes = []
    for axes, g, (R, C), (pr, pc), cs in geometry(plan):
        shapes += [pltpu.VMEM((pr, pc), jnp.float32), pltpu.VMEM((pr, pc), jnp.bfloat16), pltpu.VMEM((g - 1, pr, pc), jnp.bfloat16)]
    return shapes

def piece(k, cs, pr, pc):
    r = (k // cs) * pr
    c = lax.rem(k, cs) * pc if cs > 1 else 0
    r = pl.multiple_of(r, 16) if not isinstance(r, int) else r
    if cs > 1: c = pl.multiple_of(c, 128)
    return r, c

def rs_send(pos, geo, s, srcb, recv, ssem, rsem):
    axes, g, _, (pr, pc), cs = geo[s]
    for n, d in enumerate(offsets(axes)):
        to = partner(pos, axes, d)
        r, c = piece(index(to, axes), cs, pr, pc)
        pltpu.make_async_remote_copy(srcb.at[pl.ds(r, pr), pl.ds(c, pc)], recv.at[n], ssem, rsem, device_id=device(to), device_id_type=MESH).start()

def wait_bytes(ref, sem):
    pltpu.make_async_copy(ref, ref, sem).wait()

def rs_sum(pos, geo, s, cur, recv, rsem):
    axes, g, _, (pr, pc), cs = geo[s]
    wait_bytes(recv, rsem)
    r, c = piece(index(pos, axes), cs, pr, pc)
    total = cur[pl.ds(r, pr), pl.ds(c, pc)]
    for n in range(g - 1):
        total = total + recv[n].astype(jnp.float32)
    return total

def regions(pos, geo):
    r0 = c0 = 0
    out = [(0, 0)]
    for axes, g, _, (pr, pc), cs in geo:
        r, c = piece(index(pos, axes), cs, pr, pc)
        r0, c0 = r0 + r, c0 + c
        out.append((pl.multiple_of(r0, 16), pl.multiple_of(c0, 128)))
    return out

def ag_send(pos, geo, regs, s, out, ssem, rsem):
    axes, g, _, (pr, pc), cs = geo[s]
    r, c = regs[s + 1]
    view = out.at[pl.ds(r, pr), pl.ds(c, pc)]
    for n, d in enumerate(offsets(axes)):
        to = partner(pos, axes, d)
        pltpu.make_async_remote_copy(view, view, ssem, rsem, device_id=device(to), device_id_type=MESH).start()


def sum_kernel(plans, *refs):
    T = len(plans)
    acc, out = refs[:T], refs[T]
    refs = refs[T + 1:]
    sbf = refs[0]; refs = refs[1:]
    geos = [geometry(p) for p in plans]
    S = len(plans[0])
    scr = []
    for t in range(T):
        scr.append([refs[3 * s:3 * s + 3] for s in range(S)]); refs = refs[3 * S:]
    ssem, rsem = refs
    pos = position()
    seen = []
    for p in plans:
        for axes in p:
            for d in offsets(axes):
                full = tuple(dict(zip(axes, d)).get(a, 0) for a in "zxyc")
                if full not in seen: seen.append(full)
    bar = pltpu.get_barrier_semaphore()
    for d in seen:
        pl.semaphore_signal(bar, inc=1, device_id=device(partner(pos, "zxyc", d)), device_id_type=MESH)
    pl.semaphore_wait(bar, len(seen))
    for t in range(T):
        sbf[t] = acc[t][...].astype(jnp.bfloat16)
        rs_send(pos, geos[t], 0, sbf.at[t], scr[t][0][2], ssem.at[t, 0], rsem.at[t, 0])
    for s in range(S):
        for t in range(T):
            cur = acc[t] if s == 0 else scr[t][s - 1][0]
            total = rs_sum(pos, geos[t], s, cur, scr[t][s][2], rsem.at[t, s])
            if s < S - 1:
                scr[t][s][0][...] = total
                scr[t][s][1][...] = total.astype(jnp.bfloat16)
                rs_send(pos, geos[t], s + 1, scr[t][s][1], scr[t][s + 1][2], ssem.at[t, s + 1], rsem.at[t, s + 1])
            else:
                regs = regions(pos, geos[t])
                pr, pc = geos[t][s][3]
                r, c = regs[-1]
                out[t, pl.ds(r, pr), pl.ds(c, pc)] = total.astype(jnp.bfloat16)
                ag_send(pos, geos[t], regs, s, out.at[t], ssem.at[t, S + s], rsem.at[t, S + s])
    for s in reversed(range(S)):
        for t in range(T):
            wait_bytes(scr[t][s][2], rsem.at[t, S + s])
            if s > 0:
                ag_send(pos, geos[t], regions(pos, geos[t]), s - 1, out.at[t], ssem.at[t, S + s - 1], rsem.at[t, S + s - 1])
    for t in range(T):
        for s in range(S):
            wait_bytes(scr[t][s][2], ssem.at[t, s])
            wait_bytes(scr[t][s][2], ssem.at[t, S + s])

def sum_over_devices(mats, plans, cid, name):
    T, S = len(plans), len(plans[0])
    scratch = [pltpu.VMEM((T, 512, 512), jnp.bfloat16)]
    for p in plans: scratch += scratch_for(p)
    scratch += [pltpu.SemaphoreType.DMA((T, 2 * S))] * 2
    return pl.pallas_call(functools.partial(sum_kernel, plans),
        out_shape=jax.ShapeDtypeStruct((T, 512, 512), jnp.bfloat16),
        in_specs=[pl.BlockSpec(memory_space=pltpu.VMEM)] * T, out_specs=pl.BlockSpec(memory_space=pltpu.VMEM),
        scratch_shapes=scratch, compiler_params=pltpu.CompilerParams(collective_id=cid, has_side_effects=True, vmem_limit_bytes=40 << 20), name=name)(*mats)


def exchange_kernel(sign, send, recv, send_sem, recv_sem):
    b, p = lax.axis_index("band"), lax.axis_index("patch")
    routes = [(o, j) for j in (4, 3, 5, 2, 6, 1, 7, 0) for o in (0, 2, 1)]
    bar = pltpu.get_barrier_semaphore()
    for o, j in routes:
        if (o, j) != (1, 0):
            tb = lax.rem(b + sign * (o - 1) + NB, NB)
            pl.semaphore_signal(bar, inc=1, device_id=(tb, lax.rem(p + j, NP)), device_id_type=MESH)
    pl.semaphore_wait(bar, 23)
    for o, j in routes:
        q = lax.rem(p + j, NP)
        tb = lax.rem(b + sign * (o - 1) + NB, NB)
        if (o, j) == (1, 0):
            pltpu.make_async_copy(send.at[o, q], recv.at[o, p], recv_sem.at[o]).start()
        else:
            pltpu.make_async_remote_copy(
                send.at[o, q], recv.at[o, p], send_sem.at[o], recv_sem.at[o],
                device_id=(tb, q), device_id_type=MESH,
            ).start()
    for o in range(3):
        wait_bytes(recv.at[o], recv_sem.at[o])
    for o in range(3):
        wait_bytes(send.at[o] if o != 1 else send.at[o, pl.ds(0, 7)], send_sem.at[o])


def exchange(rows, sign, cid):
    return pl.pallas_call(
        functools.partial(exchange_kernel, sign),
        out_shape=jax.ShapeDtypeStruct(rows.shape, rows.dtype),
        in_specs=[pl.BlockSpec(memory_space=pltpu.VMEM)],
        out_specs=pl.BlockSpec(memory_space=pltpu.VMEM),
        scratch_shapes=[pltpu.SemaphoreType.DMA((3,)), pltpu.SemaphoreType.DMA((3,))],
        compiler_params=pltpu.CompilerParams(
            collective_id=cid, has_side_effects=True, vmem_limit_bytes=16 << 20
        ),
    )(rows)


def product(left, right):
    return jnp.dot(left, right, preferred_element_type=jnp.float32)


def product_back(left, weight):
    return lax.dot_general(
        left, weight, (((1,), (1,)), ((), ())), preferred_element_type=jnp.float32
    )


def outer_sum(left, right):
    return lax.dot_general(
        left, right, (((0,), (0,)), ((), ())), preferred_element_type=jnp.float32
    )


def silu_slope(value):
    sigma = jax.nn.sigmoid(value)
    return sigma * (1.0 + value * (1.0 - sigma))


def per_device(
    grid_latent,
    mesh_latent,
    grid_cotangent,
    enc_w_send,
    enc_w_recv,
    enc_w_out,
    dec_w_send,
    dec_w_recv,
    dec_w_out,
    enc_sender,
    enc_receiver,
    enc_count,
    dec_sender,
    dec_receiver,
    dec_count,
):
    bands = lax.axis_size("band")
    patches = lax.axis_size("patch")
    devices = bands * patches
    width = grid_latent.shape[1]
    grid_nodes = grid_latent.shape[0]
    mesh_nodes = mesh_latent.shape[0]
    slots = enc_sender.shape[3]
    flat = 3 * patches * slots
    slot_ids = jnp.arange(slots, dtype=jnp.int32)
    enc_live = (slot_ids[None, None, :] < enc_count[0][:, :, None]).reshape(flat, 1)
    dec_live = (slot_ids[None, None, :] < dec_count[0][:, :, None]).reshape(flat, 1)
    enc_source = enc_sender[0].reshape(flat)
    enc_target = enc_receiver[0].reshape(flat)
    dec_source = dec_sender[0].reshape(flat)
    dec_target = dec_receiver[0].reshape(flat)
    sender_rows = exchange(grid_latent[enc_sender[0]], 1, 0).reshape(flat, width)
    receiver_rows = mesh_latent[enc_target]
    enc_pre = product(sender_rows, enc_w_send) + product(receiver_rows, enc_w_recv)
    enc_act = jax.nn.silu(enc_pre).astype(jnp.bfloat16)
    enc_msg = jnp.where(enc_live, product(enc_act, enc_w_out), jnp.float32(0.0))
    mesh_new = (
        mesh_latent.astype(jnp.float32) + jax.ops.segment_sum(enc_msg, enc_target, mesh_nodes)
    ).astype(jnp.bfloat16)
    mesh_rows = exchange(mesh_new[dec_sender[0]], 1, 1).reshape(flat, width)
    grid_rows = grid_latent[dec_target]
    dec_pre = product(mesh_rows, dec_w_send) + product(grid_rows, dec_w_recv)
    dec_act = jax.nn.silu(dec_pre).astype(jnp.bfloat16)
    dec_gmsg = jnp.where(dec_live, grid_cotangent[dec_target], jnp.zeros((), jnp.bfloat16))
    dec_dpre = (product_back(dec_gmsg, dec_w_out) * silu_slope(dec_pre)).astype(jnp.bfloat16)
    dec_dsend = (
        product_back(dec_dpre, dec_w_send).astype(jnp.bfloat16).reshape(3, patches, slots, width)
    )
    mesh_return = exchange(dec_dsend, -1, 2).reshape(flat, width)
    grid_from_decoder = jax.ops.segment_sum(
        product_back(dec_dpre, dec_w_recv), dec_target, grid_nodes
    )
    grad_dec_send = outer_sum(mesh_rows, dec_dpre)
    grad_dec_recv = outer_sum(grid_rows, dec_dpre)
    grad_dec_out = outer_sum(dec_act, dec_gmsg)
    mesh_grad_new = jax.ops.segment_sum(mesh_return.astype(jnp.float32), dec_source, mesh_nodes)
    enc_gmsg = jnp.where(
        enc_live, mesh_grad_new.astype(jnp.bfloat16)[enc_target], jnp.zeros((), jnp.bfloat16)
    )
    enc_dpre = (product_back(enc_gmsg, enc_w_out) * silu_slope(enc_pre)).astype(jnp.bfloat16)
    enc_dsend = (
        product_back(enc_dpre, enc_w_send).astype(jnp.bfloat16).reshape(3, patches, slots, width)
    )
    grid_return = exchange(enc_dsend, -1, 3).reshape(flat, width)
    mesh_grad = mesh_grad_new + jax.ops.segment_sum(
        product_back(enc_dpre, enc_w_recv), enc_target, mesh_nodes
    )
    grad_enc_send = outer_sum(sender_rows, enc_dpre)
    grad_enc_recv = outer_sum(receiver_rows, enc_dpre)
    grad_enc_out = outer_sum(enc_act, enc_gmsg)
    grid_grad = grid_cotangent.astype(jnp.float32) + grid_from_decoder
    grid_grad = grid_grad + jax.ops.segment_sum(
        grid_return.astype(jnp.float32), enc_source, grid_nodes
    )
    factor = float(devices * 3 * patches * slots) ** (-0.5)
    plans = [("c", "y", "xz"), ("c", "x", "zy"), ("c", "z", "yx")] * 2
    grads = [grad_enc_send, grad_enc_recv, grad_enc_out, grad_dec_send, grad_dec_recv, grad_dec_out]
    totals = sum_over_devices(grads, plans, 4, "gradients").astype(jnp.float32) * factor
    return (grid_grad, mesh_grad, totals[0], totals[1], totals[2], totals[3], totals[4], totals[5])


def solution(mesh):
    in_specs = (
        P(("band", "patch"), None),
        P(("band", "patch"), None),
        P(("band", "patch"), None),
        P(),
        P(),
        P(),
        P(),
        P(),
        P(),
        P(("band", "patch"), None, None, None),
        P(("band", "patch"), None, None, None),
        P(("band", "patch"), None, None),
        P(("band", "patch"), None, None, None),
        P(("band", "patch"), None, None, None),
        P(("band", "patch"), None, None),
    )
    out_specs = (
        P(("band", "patch"), None),
        P(("band", "patch"), None),
        P(),
        P(),
        P(),
        P(),
        P(),
        P(),
    )
    return jax.shard_map(
        per_device, mesh=mesh, in_specs=in_specs, out_specs=out_specs, check_vma=False
    )
```

```python
import functools
import itertools

import jax
import jax.numpy as jnp
from jax import lax
from jax.experimental import pallas as pl
from jax.experimental.pallas import tpu as pltpu
from jax.sharding import PartitionSpec as P


MESH = pl.DeviceIdType.MESH
NB, NP = 16, 8
SIZES = {"z": 4, "x": 4, "y": 4, "c": 2}

def position():
    b, p = lax.axis_index("band"), lax.axis_index("patch")
    return {"z": b // 4, "x": lax.rem(b, 4), "y": p // 2, "c": lax.rem(p, 2)}

def device(pos):
    return (pos["z"] * 4 + pos["x"], pos["y"] * 2 + pos["c"])

def offsets(axes):
    return [d for d in itertools.product(*[range(SIZES[a]) for a in axes]) if any(d)]

def partner(pos, axes, d):
    new = dict(pos)
    for a, k in zip(axes, d):
        new[a] = lax.rem(pos[a] + k, SIZES[a])
    return new

def index(pos, axes):
    i = 0
    for a in axes:
        i = i * SIZES[a] + pos[a]
    return i

def geometry(plan):
    R = C = 512
    out = []
    for axes in plan:
        g = 1
        for a in axes:
            g *= SIZES[a]
        rs = min(g, R // 16)
        cs = g // rs
        out.append((axes, g, (R, C), (R // rs, C // cs), cs))
        R, C = R // rs, C // cs
    return out

def scratch_for(plan):
    shapes = []
    for axes, g, (R, C), (pr, pc), cs in geometry(plan):
        shapes += [pltpu.VMEM((pr, pc), jnp.float32), pltpu.VMEM((pr, pc), jnp.bfloat16), pltpu.VMEM((g - 1, pr, pc), jnp.bfloat16)]
    return shapes

def piece(k, cs, pr, pc):
    r = (k // cs) * pr
    c = lax.rem(k, cs) * pc if cs > 1 else 0
    r = pl.multiple_of(r, 16) if not isinstance(r, int) else r
    if cs > 1: c = pl.multiple_of(c, 128)
    return r, c

def rs_send(pos, geo, s, srcb, recv, ssem, rsem):
    axes, g, _, (pr, pc), cs = geo[s]
    for n, d in enumerate(offsets(axes)):
        to = partner(pos, axes, d)
        r, c = piece(index(to, axes), cs, pr, pc)
        pltpu.make_async_remote_copy(srcb.at[pl.ds(r, pr), pl.ds(c, pc)], recv.at[n], ssem, rsem, device_id=device(to), device_id_type=MESH).start()

def wait_bytes(ref, sem):
    pltpu.make_async_copy(ref, ref, sem).wait()

def rs_sum(pos, geo, s, cur, recv, rsem):
    axes, g, _, (pr, pc), cs = geo[s]
    wait_bytes(recv, rsem)
    r, c = piece(index(pos, axes), cs, pr, pc)
    total = cur[pl.ds(r, pr), pl.ds(c, pc)]
    for n in range(g - 1):
        total = total + recv[n].astype(jnp.float32)
    return total

def regions(pos, geo):
    r0 = c0 = 0
    out = [(0, 0)]
    for axes, g, _, (pr, pc), cs in geo:
        r, c = piece(index(pos, axes), cs, pr, pc)
        r0, c0 = r0 + r, c0 + c
        out.append((pl.multiple_of(r0, 16), pl.multiple_of(c0, 128)))
    return out

def ag_send(pos, geo, regs, s, out, ssem, rsem):
    axes, g, _, (pr, pc), cs = geo[s]
    r, c = regs[s + 1]
    view = out.at[pl.ds(r, pr), pl.ds(c, pc)]
    for n, d in enumerate(offsets(axes)):
        to = partner(pos, axes, d)
        pltpu.make_async_remote_copy(view, view, ssem, rsem, device_id=device(to), device_id_type=MESH).start()


F32, BF16 = jnp.float32, jnp.bfloat16
ORDER = (1, 0, 2)
HOPS = (4, 3, 5, 2, 6, 1, 7, 0)
PLANS = [("c", "y", "xz"), ("c", "x", "zy"), ("c", "z", "yx")]
GEO = [geometry(plan) for plan in PLANS]
STAGES = 3
DEC, ENC = 0, 3


def dot(left, right):
    return jnp.dot(left, right, preferred_element_type=F32)


def dot_back(left, weight):
    return lax.dot_general(left, weight, (((1,), (1,)), ((), ())), preferred_element_type=F32)


def outer(left, right):
    return lax.dot_general(left, right, (((0,), (0,)), ((), ())), preferred_element_type=F32)


def split(value):
    high = value.astype(BF16)
    return high, (value - high.astype(F32)).astype(BF16)


def sigmoid(value):
    return 1.0 / (1.0 + jnp.exp(-value))


def chunk(o):
    return pl.ds(o * 256, 256)


def pick(ref, o, rows, count=None):
    columns = jnp.transpose(ref[0, o])
    parts = []
    for q in range(NP):
        column = columns[:, q : q + 1]
        hit = lax.broadcasted_iota(jnp.int32, (32, rows), 1) == column
        if count is not None:
            slot = lax.broadcasted_iota(jnp.int32, (32, rows), 0)
            hit = hit & (slot < count[0, o, q])
        parts.append(jnp.where(hit, 1.0, 0.0).astype(BF16))
    return jnp.concatenate(parts, axis=0)


def edge_send(sign, o, b, p, send, recv, send_sem, recv_sem):
    band = lax.rem(b + sign * (o - 1) + NB, NB)
    for j in HOPS:
        q = lax.rem(p + j, NP)
        src = send.at[o, pl.ds(pl.multiple_of(q * 32, 32), 32)]
        dst = recv.at[o, pl.ds(pl.multiple_of(p * 32, 32), 32)]
        if o == 1 and j == 0:
            pltpu.make_async_copy(src, dst, recv_sem.at[o]).start()
        else:
            pltpu.make_async_remote_copy(
                src, dst, send_sem.at[o], recv_sem.at[o],
                device_id=(band, q), device_id_type=MESH,
            ).start()


def greet(b, p, pos):
    bar = pltpu.get_barrier_semaphore()
    n = 0
    for o in range(3):
        band = lax.rem(b + o - 1 + NB, NB)
        for j in HOPS:
            if (o, j) != (1, 0):
                pl.semaphore_signal(
                    bar, inc=1, device_id=(band, lax.rem(p + j, NP)), device_id_type=MESH
                )
                n += 1
    seen = []
    for plan in PLANS:
        for axes in plan:
            for d in offsets(axes):
                full = tuple(dict(zip(axes, d)).get(a, 0) for a in "zxyc")
                if full not in seen:
                    seen.append(full)
    for d in seen:
        pl.semaphore_signal(
            bar, inc=1, device_id=device(partner(pos, "zxyc", d)), device_id_type=MESH
        )
    return bar, n + len(seen)


class Sum:
    def __init__(self, pos, t, acc, sbf, scr, out, ssem, rsem):
        self.pos, self.geo = pos, GEO[t % 3]
        self.acc, self.sbf, self.out = acc.at[t], sbf.at[t], out[t]
        self.scr = scr[t]
        self.ssem, self.rsem = ssem, rsem
        self.t = t

    def begin(self):
        pos, geo = self.pos, self.geo
        other = pl.ds(pl.multiple_of((1 - pos["c"]) * 256, 256), 256)
        self.sbf[other, :] = self.acc[other, :].astype(BF16)
        rs_send(pos, geo, 0, self.sbf, self.scr[0][2], self.ssem.at[self.t, 0], self.rsem.at[self.t, 0])

    def reduce(self, s):
        pos, geo, scr, t = self.pos, self.geo, self.scr, self.t
        cur = self.acc if s == 0 else scr[s - 1][0]
        total = rs_sum(pos, geo, s, cur, scr[s][2], self.rsem.at[t, s])
        if s < STAGES - 1:
            scr[s][0][...] = total
            scr[s][1][...] = total.astype(BF16)
            rs_send(pos, geo, s + 1, scr[s][1], scr[s + 1][2], self.ssem.at[t, s + 1], self.rsem.at[t, s + 1])
        else:
            pr, pc = geo[s][3]
            r, c = regions(pos, geo)[-1]
            self.out[pl.ds(r, pr), pl.ds(c, pc)] = total.astype(BF16)
            self.spread(s)

    def spread(self, s):
        ag_send(self.pos, self.geo, regions(self.pos, self.geo), s, self.out,
                self.ssem.at[self.t, STAGES + s], self.rsem.at[self.t, STAGES + s])

    def gather(self, s):
        wait_bytes(self.scr[s][2], self.rsem.at[self.t, STAGES + s])
        if s > 0:
            self.spread(s - 1)

    def end(self):
        for s in range(STAGES):
            wait_bytes(self.scr[s][2], self.ssem.at[self.t, s])
            wait_bytes(self.scr[s][2], self.ssem.at[self.t, STAGES + s])


def kernel(
    grid, mesh, cot, w_es, w_er, w_eo, w_ds, w_dr, w_do,
    i_es, i_er, n_e, i_ds, i_dr, n_d,
    grid_out, mesh_out, o0, o1, o2, o3, o4, o5,
    send, recv, oh_es, oh_er, oh_ds, oh_dr, t_es, t_er, t_ds, t_dr,
    enc_pre, dec_pre, dec_back, enc_d, dec_d, acc, sbf, *rest,
):
    scr = []
    for t in range(6):
        n = 9 * t
        scr.append([rest[n + 3 * s : n + 3 * s + 3] for s in range(STAGES)])
    esend, erecv, ssem, rsem = rest[54:]
    outs = [o3, o4, o5, o0, o1, o2]
    b, p = lax.axis_index("band"), lax.axis_index("patch")
    pos = position()
    bar, greeted = greet(b, p, pos)

    def edges(phase, sign, o):
        edge_send(sign, o, b, p, send.at[phase], recv.at[phase], esend.at[phase], erecv.at[phase])

    def arrive(phase, o):
        wait_bytes(recv.at[phase, o], erecv.at[phase, o])

    sums = [Sum(pos, t, acc, sbf, scr, outs, ssem, rsem) for t in range(6)]
    dec_sums, enc_sums = sums[:3], sums[3:]

    for n, o in enumerate(ORDER):
        oh_es[chunk(o), :] = pick(i_es, o, 256)
        send[0, o] = dot(oh_es[chunk(o), :], grid[...]).astype(BF16)
        if n == 0:
            pl.semaphore_wait(bar, greeted)
        edges(0, 1, o)

    for o in range(3):
        oh_er[chunk(o), :] = pick(i_er, o, 128, n_e)
        t_er[:, chunk(o)] = jnp.transpose(oh_er[chunk(o), :])
    high, low = split(dot(mesh[...], w_er[...]))
    for o in range(3):
        enc_pre[chunk(o), :] = dot(oh_er[chunk(o), :], high) + dot(oh_er[chunk(o), :], low)
    for o in range(3):
        oh_ds[chunk(o), :] = pick(i_ds, o, 128)
        t_ds[:, chunk(o)] = jnp.transpose(oh_ds[chunk(o), :])
        oh_dr[chunk(o), :] = pick(i_dr, o, 256, n_d)
        t_dr[:, chunk(o)] = jnp.transpose(oh_dr[chunk(o), :])
        t_es[:, chunk(o)] = jnp.transpose(oh_es[chunk(o), :])
    high, low = split(dot(grid[...], w_dr[...]))
    for o in range(3):
        dec_pre[chunk(o), :] = dot(oh_dr[chunk(o), :], high) + dot(oh_dr[chunk(o), :], low)
    high, low = split(dot_back(cot[...], w_do[...]))
    for o in range(3):
        dec_back[chunk(o), :] = dot(oh_dr[chunk(o), :], high) + dot(oh_dr[chunk(o), :], low)

    enc_sum = None
    for o in ORDER:
        arrive(0, o)
        pre = dot(recv[0, o], w_es[...]) + enc_pre[chunk(o), :]
        enc_pre[chunk(o), :] = pre
        act = (pre * sigmoid(pre)).astype(BF16)
        part = dot(t_er[:, chunk(o)], act)
        enc_sum = part if enc_sum is None else enc_sum + part
    high, low = split(enc_sum)
    mesh_new = (mesh[...].astype(F32) + (dot(high, w_eo[...]) + dot(low, w_eo[...]))).astype(BF16)

    for o in ORDER:
        send[1, o] = dot(oh_ds[chunk(o), :], mesh_new).astype(BF16)
        edges(1, 1, o)
    for o in range(3):
        pre = enc_pre[chunk(o), :]
        sigma = sigmoid(pre)
        enc_pre[chunk(o), :] = sigma * (1.0 + pre * (1.0 - sigma))
    enc_act_sum = high

    act_sum = None
    for o in ORDER:
        arrive(1, o)
        pre = dot(recv[1, o], w_ds[...]) + dec_pre[chunk(o), :]
        sigma = sigmoid(pre)
        slope = sigma * (1.0 + pre * (1.0 - sigma))
        dpre = (dec_back[chunk(o), :] * slope).astype(BF16)
        dec_d[chunk(o), :] = dpre
        send[2, o] = dot_back(dpre, w_ds[...]).astype(BF16)
        edges(2, -1, o)
        part = dot(t_dr[:, chunk(o)], (pre * sigma).astype(BF16))
        act_sum = part if act_sum is None else act_sum + part

    acc[DEC + 0] = outer(recv[1].reshape(768, 512), dec_d[...])
    dec_sums[0].begin()
    grid_sum = dot(t_dr[...], dec_d[...]).astype(BF16)
    acc[DEC + 1] = outer(grid[...], grid_sum)
    dec_sums[1].begin()
    acc[DEC + 2] = outer(act_sum.astype(BF16), cot[...])
    dec_sums[2].begin()
    grid_out[...] = cot[...].astype(F32) + dot_back(grid_sum, w_dr[...])
    for one in dec_sums:
        one.reduce(0)

    mesh_back = None
    for o in ORDER:
        arrive(2, o)
        part = dot(t_ds[:, chunk(o)], recv[2, o])
        mesh_back = part if mesh_back is None else mesh_back + part
    gmsg = mesh_back.astype(BF16)
    high, low = split(dot_back(gmsg, w_eo[...]))
    for o in ORDER:
        back = dot(oh_er[chunk(o), :], high) + dot(oh_er[chunk(o), :], low)
        enc_d[chunk(o), :] = (back * enc_pre[chunk(o), :]).astype(BF16)
    acc[ENC + 0] = outer(recv[0].reshape(768, 512), enc_d[...])
    enc_sums[0].begin()
    mesh_sum = dot(t_er[...], enc_d[...]).astype(BF16)
    acc[ENC + 1] = outer(mesh[...], mesh_sum)
    enc_sums[1].begin()
    acc[ENC + 2] = outer(enc_act_sum, gmsg)
    enc_sums[2].begin()
    for o in ORDER:
        send[3, o] = dot_back(enc_d[chunk(o), :], w_es[...]).astype(BF16)
        edges(3, -1, o)
    mesh_out[...] = mesh_back + dot_back(mesh_sum, w_er[...])

    for one in enc_sums:
        one.reduce(0)
    for one in dec_sums:
        one.reduce(1)
    for one in enc_sums:
        one.reduce(1)
    for one in dec_sums:
        one.reduce(2)
    for one in enc_sums:
        one.reduce(2)
    total = grid_out[...]
    for o in ORDER:
        arrive(3, o)
        total = total + dot(t_es[:, chunk(o)], recv[3, o])
    grid_out[...] = total
    for s in reversed(range(STAGES)):
        for one in dec_sums + enc_sums:
            one.gather(s)

    for phase in range(4):
        for o in range(3):
            sent = send.at[phase, o] if o != 1 else send.at[phase, o, pl.ds(0, 224)]
            wait_bytes(sent, esend.at[phase, o])
    for one in sums:
        one.end()


def per_device(
    grid_latent, mesh_latent, grid_cotangent,
    enc_w_send, enc_w_recv, enc_w_out, dec_w_send, dec_w_recv, dec_w_out,
    enc_sender, enc_receiver, enc_count, dec_sender, dec_receiver, dec_count,
):
    vmem = pl.BlockSpec(memory_space=pltpu.VMEM)
    smem = pl.BlockSpec(memory_space=pltpu.SMEM)
    scratch = [
        pltpu.VMEM((4, 3, 256, 512), BF16),
        pltpu.VMEM((4, 3, 256, 512), BF16),
        pltpu.VMEM((768, 256), BF16),
        pltpu.VMEM((768, 128), BF16),
        pltpu.VMEM((768, 128), BF16),
        pltpu.VMEM((768, 256), BF16),
        pltpu.VMEM((256, 768), BF16),
        pltpu.VMEM((128, 768), BF16),
        pltpu.VMEM((128, 768), BF16),
        pltpu.VMEM((256, 768), BF16),
        pltpu.VMEM((768, 512), F32),
        pltpu.VMEM((768, 512), F32),
        pltpu.VMEM((768, 512), F32),
        pltpu.VMEM((768, 512), BF16),
        pltpu.VMEM((768, 512), BF16),
        pltpu.VMEM((6, 512, 512), F32),
        pltpu.VMEM((6, 512, 512), BF16),
    ]
    for t in range(6):
        scratch += scratch_for(PLANS[t % 3])
    scratch += [pltpu.SemaphoreType.DMA((4, 3))] * 2
    scratch += [pltpu.SemaphoreType.DMA((6, 2 * STAGES))] * 2
    square = jax.ShapeDtypeStruct((512, 512), BF16)
    results = pl.pallas_call(
        kernel,
        out_shape=[
            jax.ShapeDtypeStruct((256, 512), F32),
            jax.ShapeDtypeStruct((128, 512), F32),
        ] + [square] * 6,
        in_specs=[vmem] * 9 + [vmem, vmem, smem, vmem, vmem, smem],
        out_specs=[vmem] * 8,
        scratch_shapes=scratch,
        compiler_params=pltpu.CompilerParams(
            collective_id=0, has_side_effects=True, vmem_limit_bytes=56 << 20
        ),
    )(
        grid_latent, mesh_latent, grid_cotangent,
        enc_w_send, enc_w_recv, enc_w_out, dec_w_send, dec_w_recv, dec_w_out,
        enc_sender, enc_receiver, enc_count, dec_sender, dec_receiver, dec_count,
    )
    factor = float(NB * NP * 3 * NP * 32) ** (-0.5)
    return (results[0], results[1]) + tuple(g.astype(F32) * factor for g in results[2:])


def solution(mesh):
    in_specs = (
        P(("band", "patch"), None),
        P(("band", "patch"), None),
        P(("band", "patch"), None),
        P(),
        P(),
        P(),
        P(),
        P(),
        P(),
        P(("band", "patch"), None, None, None),
        P(("band", "patch"), None, None, None),
        P(("band", "patch"), None, None),
        P(("band", "patch"), None, None, None),
        P(("band", "patch"), None, None, None),
        P(("band", "patch"), None, None),
    )
    out_specs = (
        P(("band", "patch"), None),
        P(("band", "patch"), None),
        P(),
        P(),
        P(),
        P(),
        P(),
        P(),
    )
    return jax.shard_map(
        per_device, mesh=mesh, in_specs=in_specs, out_specs=out_specs, check_vma=False
    )
```

```python
import functools
import itertools

import jax
import jax.numpy as jnp
from jax import lax
from jax.experimental import pallas as pl
from jax.experimental.pallas import tpu as pltpu
from jax.sharding import PartitionSpec as P


MESH = pl.DeviceIdType.MESH
NB, NP = 16, 8
SIZES = {"z": 4, "x": 4, "y": 4, "c": 2}

def position():
    b, p = lax.axis_index("band"), lax.axis_index("patch")
    return {"z": b // 4, "x": lax.rem(b, 4), "y": p // 2, "c": lax.rem(p, 2)}

def device(pos):
    return (pos["z"] * 4 + pos["x"], pos["y"] * 2 + pos["c"])

def offsets(axes):
    return [d for d in itertools.product(*[range(SIZES[a]) for a in axes]) if any(d)]

def partner(pos, axes, d):
    new = dict(pos)
    for a, k in zip(axes, d):
        new[a] = lax.rem(pos[a] + k, SIZES[a])
    return new

def index(pos, axes):
    i = 0
    for a in axes:
        i = i * SIZES[a] + pos[a]
    return i

def geometry(plan):
    R = C = 512
    out = []
    for axes in plan:
        g = 1
        for a in axes:
            g *= SIZES[a]
        rs = min(g, R // 16)
        cs = g // rs
        out.append((axes, g, (R, C), (R // rs, C // cs), cs))
        R, C = R // rs, C // cs
    return out

def scratch_for(plan):
    shapes = []
    for axes, g, (R, C), (pr, pc), cs in geometry(plan):
        shapes += [pltpu.VMEM((pr, pc), jnp.float32), pltpu.VMEM((pr, pc), jnp.bfloat16), pltpu.VMEM((g - 1, pr, pc), jnp.bfloat16)]
    return shapes

def piece(k, cs, pr, pc):
    r = (k // cs) * pr
    c = lax.rem(k, cs) * pc if cs > 1 else 0
    r = pl.multiple_of(r, 16) if not isinstance(r, int) else r
    if cs > 1: c = pl.multiple_of(c, 128)
    return r, c

def rs_send(pos, geo, s, srcb, recv, ssem, rsem):
    axes, g, _, (pr, pc), cs = geo[s]
    for n, d in enumerate(offsets(axes)):
        to = partner(pos, axes, d)
        r, c = piece(index(to, axes), cs, pr, pc)
        pltpu.make_async_remote_copy(srcb.at[pl.ds(r, pr), pl.ds(c, pc)], recv.at[n], ssem, rsem, device_id=device(to), device_id_type=MESH).start()

def wait_bytes(ref, sem):
    pltpu.make_async_copy(ref, ref, sem).wait()

def rs_sum(pos, geo, s, cur, recv, rsem):
    axes, g, _, (pr, pc), cs = geo[s]
    wait_bytes(recv, rsem)
    r, c = piece(index(pos, axes), cs, pr, pc)
    total = cur[pl.ds(r, pr), pl.ds(c, pc)]
    for n in range(g - 1):
        total = total + recv[n].astype(jnp.float32)
    return total

def regions(pos, geo):
    r0 = c0 = 0
    out = [(0, 0)]
    for axes, g, _, (pr, pc), cs in geo:
        r, c = piece(index(pos, axes), cs, pr, pc)
        r0, c0 = r0 + r, c0 + c
        out.append((pl.multiple_of(r0, 16), pl.multiple_of(c0, 128)))
    return out

def ag_send(pos, geo, regs, s, out, ssem, rsem):
    axes, g, _, (pr, pc), cs = geo[s]
    r, c = regs[s + 1]
    view = out.at[pl.ds(r, pr), pl.ds(c, pc)]
    for n, d in enumerate(offsets(axes)):
        to = partner(pos, axes, d)
        pltpu.make_async_remote_copy(view, view, ssem, rsem, device_id=device(to), device_id_type=MESH).start()


F32, BF16 = jnp.float32, jnp.bfloat16
OUT_ORDER = (2, 1, 3, 0)
IN_ORDER = (2, 1, 3, 0)
TAIL = (
    "s", "e0", "m", "d1", "e1", "d2", "e2", "d3", "R2", "e3", "R1", "R3", "R0",
    "e4", "d4", "e5", "d5", "g",
)
BLOCKS = [(o, dc) for o in range(3) for dc in range(2)]
ROWS = 32 * len(BLOCKS)
PLANS = [
    ("c", "z", "xy"), ("c", "x", "zy"), ("c", "z", "xy"),
    ("c", "y", "xz"), ("c", "x", "zy"), ("c", "z", "xy"),
]
GEO = [geometry(plan) for plan in PLANS]
FACTOR = float(NB * NP * 3 * NP * 32) ** (-0.5)
STAGES = 3
DEC, ENC = 0, 3


def dot(left, right):
    return jnp.dot(left, right, preferred_element_type=F32)


def dot_back(left, weight):
    return lax.dot_general(left, weight, (((1,), (1,)), ((), ())), preferred_element_type=F32)


def outer(left, right):
    return lax.dot_general(left, right, (((0,), (0,)), ((), ())), preferred_element_type=F32)


def split(value):
    high = value.astype(BF16)
    return high, (value - high.astype(F32)).astype(BF16)


def sigmoid(value):
    return 1.0 / (1.0 + jnp.exp(-value))


def chunk(dy):
    return pl.ds(dy * ROWS, ROWS)


def patch_at(pos, sign, dy, dc):
    return lax.rem(pos["y"] + sign * dy + 4, 4) * 2 + lax.rem(pos["c"] + dc, 2)


def live_only(ref, count, o):
    columns = jnp.transpose(ref[0, o])
    slot = lax.broadcasted_iota(jnp.int32, (32, NP), 0)
    return jnp.transpose(jnp.where(slot < count[o], columns, -1))


def pick(row_of, pos, sign, dy, rows):
    lines = [row_of(o, patch_at(pos, sign, dy, dc)) for o, dc in BLOCKS]
    columns = jnp.transpose(jnp.concatenate(lines + lines[:2], axis=0))
    node = lax.broadcasted_iota(jnp.int32, (32, rows), 1)
    parts = []
    for n in range(len(BLOCKS)):
        parts.append(jnp.where(node == columns[:, n : n + 1], 1.0, 0.0).astype(BF16))
    return jnp.concatenate(parts, axis=0)


def edge_send(sign, dy, b, pos, send, recv, send_sem, recv_sem):
    for n, (o, dc) in enumerate(BLOCKS):
        band = lax.rem(b + sign * (o - 1) + NB, NB)
        src = send.at[dy, pl.ds(n * 32, 32)]
        dst = recv.at[dy, pl.ds(n * 32, 32)]
        if (o, dy, dc) == (1, 0, 0):
            pltpu.make_async_copy(src, dst, recv_sem.at[dy]).start()
        else:
            pltpu.make_async_remote_copy(
                src, dst, send_sem.at[dy], recv_sem.at[dy],
                device_id=(band, patch_at(pos, sign, dy, dc)), device_id_type=MESH,
            ).start()


def greet(b, p, pos):
    bar = pltpu.get_barrier_semaphore()
    n = 0
    for dy in OUT_ORDER:
        for o, dc in BLOCKS:
            if (o, dy, dc) != (1, 0, 0):
                band = lax.rem(b + o - 1 + NB, NB)
                pl.semaphore_signal(
                    bar, inc=1, device_id=(band, patch_at(pos, 1, dy, dc)), device_id_type=MESH
                )
                n += 1
    seen = []
    for plan in PLANS:
        for axes in plan:
            for d in offsets(axes):
                full = tuple(dict(zip(axes, d)).get(a, 0) for a in "zxyc")
                if full not in seen:
                    seen.append(full)
    for d in seen:
        pl.semaphore_signal(
            bar, inc=1, device_id=device(partner(pos, "zxyc", d)), device_id_type=MESH
        )
    return bar, n + len(seen)


class Sum:
    def __init__(self, pos, t, acc, sbf, scr, out, ssem, rsem):
        self.pos, self.geo = pos, GEO[t]
        self.acc, self.sbf, self.out = acc.at[t], sbf.at[t], out.at[t]
        self.scr, self.t = scr[t], t
        self.ssem, self.rsem = ssem, rsem
        self.sibling = partner(pos, "c", (1,))
        self.axis = PLANS[t][1]
        self.half = pos["c"] * 256

    def begin(self):
        other = pl.ds(pl.multiple_of((1 - self.pos["c"]) * 256, 256), 256)
        self.sbf[other, :] = self.acc[other, :].astype(BF16)
        rs_send(self.pos, self.geo, 0, self.sbf, self.scr[0][2],
                self.ssem.at[self.t, 0], self.rsem.at[self.t, 0])

    def reduce(self, s):
        pos, geo, scr, t = self.pos, self.geo, self.scr, self.t
        cur = self.acc if s == 0 else scr[s - 1][0]
        total = rs_sum(pos, geo, s, cur, scr[s][2], self.rsem.at[t, s])
        if s < 2:
            scr[s][0][...] = total
            scr[s][1][...] = total.astype(BF16)
            rs_send(pos, geo, s + 1, scr[s][1], scr[s + 1][2],
                    self.ssem.at[t, s + 1], self.rsem.at[t, s + 1])
        else:
            pr, pc = geo[s][3]
            regs = regions(pos, geo)
            r, c = regs[-1]
            self.out[pl.ds(r, pr), pl.ds(c, pc)] = total.astype(BF16)
            ag_send(pos, geo, regs, 2, self.out, self.ssem.at[t, 4], self.rsem.at[t, 4])

    def rows(self, k):
        place = lax.rem(self.pos[self.axis] - k + 4, 4)
        return self.out.at[pl.ds(pl.multiple_of(self.half + place * 64, 64), 64), :]

    def pass_on(self, k):
        view = self.rows(k)
        pltpu.make_async_remote_copy(
            view, view, self.ssem.at[self.t, 3], self.rsem.at[self.t, 3],
            device_id=device(self.sibling), device_id_type=MESH,
        ).start()

    def gather_plane(self):
        t = self.t
        wait_bytes(self.scr[2][2], self.rsem.at[t, 4])
        view = self.rows(0)
        for d in (2, 1, 3):
            to = partner(self.pos, self.axis, (d,))
            pltpu.make_async_remote_copy(
                view, view, self.ssem.at[t, 5], self.rsem.at[t, 4 + d],
                device_id=device(to), device_id_type=MESH,
            ).start()
        self.pass_on(0)

    def gather_axis(self, d):
        wait_bytes(self.rows(d), self.rsem.at[self.t, 4 + d])
        self.pass_on(d)

    def gather_pair(self):
        wait_bytes(self.scr[0][2], self.rsem.at[self.t, 3])

    def end(self):
        t, scr = self.t, self.scr
        for place, ref in enumerate((scr[0], scr[1], scr[2], scr[0], scr[2], scr[1])):
            wait_bytes(ref[2], self.ssem.at[t, place])


def kernel(
    grid, mesh_in, cot_in, es_in, er_in, eo_in, ds_in, dr_in, do_in,
    i_es, i_er, n_e, i_ds, i_dr, n_d,
    grid_res, mesh_res, o0, o1, o2, o3, o4, o5,
    mesh, cot, w_es, w_er, w_eo, w_ds, w_dr, w_do, grid_out, mesh_out, out,
    isem, osem, live, send, recv, oh_es, oh_er, oh_ds, oh_dr, t_es, t_er, t_ds, t_dr,
    enc_pre, dec_pre, dec_back, enc_d, dec_d, acc, sbf, *rest,
):
    scr = []
    for t in range(6):
        n = 9 * t
        scr.append([rest[n + 3 * s : n + 3 * s + 3] for s in range(STAGES)])
    esend, erecv, ssem, rsem = rest[54:]
    results = [o3, o4, o5, o0, o1, o2]
    loads = {}
    for n, (name, src, dst) in enumerate((
        ("er", er_in, w_er), ("mesh", mesh_in, mesh), ("dr", dr_in, w_dr), ("cot", cot_in, cot),
        ("do", do_in, w_do), ("es", es_in, w_es), ("eo", eo_in, w_eo), ("ds", ds_in, w_ds),
    )):
        loads[name] = pltpu.make_async_copy(src, dst, isem.at[n])
        loads[name].start()

    def store(n, src, dst):
        copy = pltpu.make_async_copy(src, dst, osem.at[n])
        copy.start()
        return copy

    b, p = lax.axis_index("band"), lax.axis_index("patch")
    pos = position()
    bar, greeted = greet(b, p, pos)

    def edges(phase, sign, dy):
        edge_send(sign, dy, b, pos, send.at[phase], recv.at[phase], esend.at[phase], erecv.at[phase])

    def arrive(phase, o):
        wait_bytes(recv.at[phase, o], erecv.at[phase, o])

    sums = [Sum(pos, t, acc, sbf, scr, out, ssem, rsem) for t in range(6)]
    dec_sums, enc_sums = sums[:3], sums[3:]

    for n, dy in enumerate(OUT_ORDER):
        oh_es[chunk(dy), :] = pick(lambda o, q: i_es[0, o, pl.ds(q, 1), :], pos, 1, dy, 256)
        send[0, dy] = dot(oh_es[chunk(dy), :], grid[...]).astype(BF16)
        if n == 0:
            pl.semaphore_wait(bar, greeted)
        edges(0, 1, dy)

    for o in range(3):
        live[0, o] = live_only(i_er, n_e, o)
        live[1, o] = live_only(i_dr, n_d, o)
    for dy in range(4):
        oh_er[chunk(dy), :] = pick(lambda o, q: live[0, o, pl.ds(q, 1), :], pos, -1, dy, 128)
    t_er[...] = jnp.transpose(oh_er[...])
    loads["er"].wait()
    loads["mesh"].wait()
    high, low = split(dot(mesh[...], w_er[...]))
    for dy in range(4):
        enc_pre[chunk(dy), :] = dot(oh_er[chunk(dy), :], high) + dot(oh_er[chunk(dy), :], low)
    for dy in range(4):
        oh_ds[chunk(dy), :] = pick(lambda o, q: i_ds[0, o, pl.ds(q, 1), :], pos, 1, dy, 128)
        oh_dr[chunk(dy), :] = pick(lambda o, q: live[1, o, pl.ds(q, 1), :], pos, -1, dy, 256)
    t_ds[...] = jnp.transpose(oh_ds[...])
    t_dr[...] = jnp.transpose(oh_dr[...])
    t_es[...] = jnp.transpose(oh_es[...])
    loads["dr"].wait()
    high, low = split(dot(grid[...], w_dr[...]))
    for dy in range(4):
        dec_pre[chunk(dy), :] = dot(oh_dr[chunk(dy), :], high) + dot(oh_dr[chunk(dy), :], low)
    loads["cot"].wait()
    loads["do"].wait()
    high, low = split(dot_back(cot[...], w_do[...]))
    for dy in range(4):
        dec_back[chunk(dy), :] = dot(oh_dr[chunk(dy), :], high) + dot(oh_dr[chunk(dy), :], low)

    for name in ("es", "eo", "ds"):
        loads[name].wait()
    for dy in IN_ORDER:
        arrive(0, dy)
        pre = dot(recv[0, dy], w_es[...]) + enc_pre[chunk(dy), :]
        enc_pre[chunk(dy), :] = pre
        enc_d[chunk(dy), :] = (pre * sigmoid(pre)).astype(BF16)
    high, low = split(dot(t_er[...], enc_d[...]))
    mesh_new = (mesh[...].astype(F32) + (dot(high, w_eo[...]) + dot(low, w_eo[...]))).astype(BF16)
    enc_act_sum = high

    for dy in OUT_ORDER:
        send[1, dy] = dot(oh_ds[chunk(dy), :], mesh_new).astype(BF16)
        edges(1, 1, dy)
    for dy in range(4):
        pre = enc_pre[chunk(dy), :]
        sigma = sigmoid(pre)
        enc_pre[chunk(dy), :] = sigma * (1.0 + pre * (1.0 - sigma))

    for dy in IN_ORDER:
        arrive(1, dy)
        pre = dot(recv[1, dy], w_ds[...]) + dec_pre[chunk(dy), :]
        sigma = sigmoid(pre)
        slope = sigma * (1.0 + pre * (1.0 - sigma))
        dpre = (dec_back[chunk(dy), :] * slope).astype(BF16)
        dec_d[chunk(dy), :] = dpre
        send[2, dy] = dot_back(dpre, w_ds[...]).astype(BF16)
        edges(2, -1, dy)
        enc_d[chunk(dy), :] = (pre * sigma).astype(BF16)

    acc[DEC + 0] = outer(recv[1].reshape(768, 512), dec_d[...])
    dec_sums[0].begin()
    grid_sum = dot(t_dr[...], dec_d[...]).astype(BF16)
    acc[DEC + 1] = outer(grid[...], grid_sum)
    dec_sums[1].begin()
    acc[DEC + 2] = outer(dot(t_dr[...], enc_d[...]).astype(BF16), cot[...])
    dec_sums[2].begin()
    grid_out[...] = cot[...].astype(F32) + dot_back(grid_sum, w_dr[...])
    for one in dec_sums:
        one.reduce(0)
    for dy in IN_ORDER:
        arrive(2, dy)
    mesh_back = dot(t_ds[...], recv[2].reshape(768, 512))
    gmsg = mesh_back.astype(BF16)
    acc[ENC + 2] = outer(enc_act_sum, gmsg)
    enc_sums[2].begin()
    high, low = split(dot_back(gmsg, w_eo[...]))
    for dy in range(4):
        back = dot(oh_er[chunk(dy), :], high) + dot(oh_er[chunk(dy), :], low)
        enc_d[chunk(dy), :] = (back * enc_pre[chunk(dy), :]).astype(BF16)
    acc[ENC + 0] = outer(recv[0].reshape(768, 512), enc_d[...])
    enc_sums[0].begin()
    mesh_sum = dot(t_er[...], enc_d[...]).astype(BF16)
    acc[ENC + 1] = outer(mesh[...], mesh_sum)
    enc_sums[1].begin()

    stores = []

    def advance(group, n):
        if n == 4:
            for d in (1, 3, 2):
                for one in group:
                    one.gather_axis(d)
            return
        for one in group:
            if n < 3:
                one.reduce(n)
            elif n == 3:
                one.gather_plane()
            else:
                one.gather_pair()
                stores.append(store(one.t, one.out, results[one.t]))

    for token in TAIL:
        if token[0] == "d":
            advance(dec_sums, int(token[1]))
        elif token[0] == "e":
            advance((enc_sums[2], enc_sums[0], enc_sums[1]), int(token[1]))
        elif token[0] == "R":
            edges(3, -1, int(token[1]))
        elif token == "s":
            for dy in OUT_ORDER:
                send[3, dy] = dot_back(enc_d[chunk(dy), :], w_es[...]).astype(BF16)
        elif token == "m":
            mesh_out[...] = mesh_back + dot_back(mesh_sum, w_er[...])
            stores.append(store(6, mesh_out, mesh_res))
        elif token == "g":
            for dy in OUT_ORDER:
                arrive(3, dy)
            grid_out[...] = grid_out[...] + dot(t_es[...], recv[3].reshape(768, 512))
            stores.append(store(7, grid_out, grid_res))

    for phase in range(4):
        for dy in range(4):
            sent = send.at[phase, dy] if dy else send.at[phase, dy, pl.ds(0, ROWS - 32)]
            wait_bytes(sent, esend.at[phase, dy])
    for one in sums:
        one.end()
    for one in stores:
        one.wait()


def finish(grid_in, mesh_in, *refs):
    sums, (grid_out, mesh_out), outs = refs[:6], refs[6:8], refs[8:14]
    narrow, wide, grid_rows, mesh_rows, in_sem, out_sem = refs[14:]
    loads = [pltpu.make_async_copy(sums[t], narrow.at[t], in_sem.at[t]) for t in range(6)]
    stores = [pltpu.make_async_copy(wide.at[t], outs[t], out_sem.at[t]) for t in range(6)]
    loads.append(pltpu.make_async_copy(grid_in, grid_rows, in_sem.at[6]))
    loads.append(pltpu.make_async_copy(mesh_in, mesh_rows, in_sem.at[7]))
    stores.append(pltpu.make_async_copy(grid_rows, grid_out, out_sem.at[6]))
    stores.append(pltpu.make_async_copy(mesh_rows, mesh_out, out_sem.at[7]))
    for n in (6, 0, 1, 2, 3, 4, 5, 7):
        loads[n].start()
    for n in (6, 7):
        loads[n].wait()
        stores[n].start()
    for t in range(6):
        loads[t].wait()
        wide[t] = narrow[t].astype(F32) * FACTOR
        stores[t].start()
    for one in stores:
        one.wait()


def per_device(
    grid_latent, mesh_latent, grid_cotangent,
    enc_w_send, enc_w_recv, enc_w_out, dec_w_send, dec_w_recv, dec_w_out,
    enc_sender, enc_receiver, enc_count, dec_sender, dec_receiver, dec_count,
):
    vmem = pl.BlockSpec(memory_space=pltpu.VMEM)
    anywhere = pl.BlockSpec(memory_space=pl.ANY)
    weight = pltpu.VMEM((512, 512), BF16)
    scratch = [
        pltpu.VMEM((128, 512), BF16),
        pltpu.VMEM((256, 512), BF16),
    ] + [weight] * 6 + [
        pltpu.VMEM((256, 512), F32),
        pltpu.VMEM((128, 512), F32),
        pltpu.VMEM((6, 512, 512), BF16),
        pltpu.SemaphoreType.DMA((8,)),
        pltpu.SemaphoreType.DMA((8,)),
        pltpu.VMEM((2, 3, NP, 32), jnp.int32),
        pltpu.VMEM((4, 4, ROWS, 512), BF16),
        pltpu.VMEM((4, 4, ROWS, 512), BF16),
        pltpu.VMEM((768, 256), BF16),
        pltpu.VMEM((768, 128), BF16),
        pltpu.VMEM((768, 128), BF16),
        pltpu.VMEM((768, 256), BF16),
        pltpu.VMEM((256, 768), BF16),
        pltpu.VMEM((128, 768), BF16),
        pltpu.VMEM((128, 768), BF16),
        pltpu.VMEM((256, 768), BF16),
        pltpu.VMEM((768, 512), F32),
        pltpu.VMEM((768, 512), F32),
        pltpu.VMEM((768, 512), F32),
        pltpu.VMEM((768, 512), BF16),
        pltpu.VMEM((768, 512), BF16),
        pltpu.VMEM((6, 512, 512), F32),
        pltpu.VMEM((6, 512, 512), BF16),
    ]
    for t in range(6):
        scratch += scratch_for(PLANS[t])
    scratch += [pltpu.SemaphoreType.DMA((4, 4))] * 2
    scratch += [pltpu.SemaphoreType.DMA((6, 6)), pltpu.SemaphoreType.DMA((6, 8))]
    square = jax.ShapeDtypeStruct((512, 512), BF16)
    rows = [jax.ShapeDtypeStruct((256, 512), F32), jax.ShapeDtypeStruct((128, 512), F32)]
    results = pl.pallas_call(
        kernel,
        out_shape=rows + [square] * 6,
        in_specs=[vmem] + [anywhere] * 8 + [vmem] * 6,
        out_specs=[anywhere] * 8,
        scratch_shapes=scratch,
        compiler_params=pltpu.CompilerParams(
            collective_id=0, has_side_effects=True, vmem_limit_bytes=56 << 20
        ),
    )(
        grid_latent, mesh_latent, grid_cotangent,
        enc_w_send, enc_w_recv, enc_w_out, dec_w_send, dec_w_recv, dec_w_out,
        enc_sender, enc_receiver, jnp.transpose(enc_count, (1, 0, 2)),
        dec_sender, dec_receiver, jnp.transpose(dec_count, (1, 0, 2)),
    )
    return pl.pallas_call(
        finish,
        out_shape=rows + [jax.ShapeDtypeStruct((512, 512), F32)] * 6,
        in_specs=[anywhere] * 8,
        out_specs=[anywhere] * 8,
        scratch_shapes=[
            pltpu.VMEM((6, 512, 512), BF16),
            pltpu.VMEM((6, 512, 512), F32),
            pltpu.VMEM((256, 512), F32),
            pltpu.VMEM((128, 512), F32),
            pltpu.SemaphoreType.DMA((8,)),
            pltpu.SemaphoreType.DMA((8,)),
        ],
        compiler_params=pltpu.CompilerParams(vmem_limit_bytes=60 << 20),
    )(*results)


def solution(mesh):
    in_specs = (
        P(("band", "patch"), None),
        P(("band", "patch"), None),
        P(("band", "patch"), None),
        P(),
        P(),
        P(),
        P(),
        P(),
        P(),
        P(("band", "patch"), None, None, None),
        P(("band", "patch"), None, None, None),
        P(("band", "patch"), None, None),
        P(("band", "patch"), None, None, None),
        P(("band", "patch"), None, None, None),
        P(("band", "patch"), None, None),
    )
    out_specs = (
        P(("band", "patch"), None),
        P(("band", "patch"), None),
        P(),
        P(),
        P(),
        P(),
        P(),
        P(),
    )
    return jax.shard_map(
        per_device, mesh=mesh, in_specs=in_specs, out_specs=out_specs, check_vma=False
    )
```

```python
import functools
import itertools

import jax
import jax.numpy as jnp
from jax import lax
from jax.experimental import pallas as pl
from jax.experimental.pallas import tpu as pltpu
from jax.sharding import PartitionSpec as P


MESH = pl.DeviceIdType.MESH
NB, NP = 16, 8
SIZES = {"z": 4, "x": 4, "y": 4, "c": 2}

def position():
    b, p = lax.axis_index("band"), lax.axis_index("patch")
    return {"z": b // 4, "x": lax.rem(b, 4), "y": p // 2, "c": lax.rem(p, 2)}

def device(pos):
    return (pos["z"] * 4 + pos["x"], pos["y"] * 2 + pos["c"])

def offsets(axes):
    return [d for d in itertools.product(*[range(SIZES[a]) for a in axes]) if any(d)]

def partner(pos, axes, d):
    new = dict(pos)
    for a, k in zip(axes, d):
        new[a] = lax.rem(pos[a] + k, SIZES[a])
    return new

def index(pos, axes):
    i = 0
    for a in axes:
        i = i * SIZES[a] + pos[a]
    return i

def geometry(plan):
    R = C = 512
    out = []
    for axes in plan:
        g = 1
        for a in axes:
            g *= SIZES[a]
        rs = min(g, R // 16)
        cs = g // rs
        out.append((axes, g, (R, C), (R // rs, C // cs), cs))
        R, C = R // rs, C // cs
    return out

def scratch_for(plan):
    shapes = []
    for axes, g, (R, C), (pr, pc), cs in geometry(plan):
        shapes += [pltpu.VMEM((pr, pc), jnp.float32), pltpu.VMEM((pr, pc), jnp.bfloat16), pltpu.VMEM((g - 1, pr, pc), jnp.bfloat16)]
    return shapes

def piece(k, cs, pr, pc):
    r = (k // cs) * pr
    c = lax.rem(k, cs) * pc if cs > 1 else 0
    r = pl.multiple_of(r, 16) if not isinstance(r, int) else r
    if cs > 1: c = pl.multiple_of(c, 128)
    return r, c

def rs_send(pos, geo, s, srcb, recv, ssem, rsem):
    axes, g, _, (pr, pc), cs = geo[s]
    for n, d in enumerate(offsets(axes)):
        to = partner(pos, axes, d)
        r, c = piece(index(to, axes), cs, pr, pc)
        pltpu.make_async_remote_copy(srcb.at[pl.ds(r, pr), pl.ds(c, pc)], recv.at[n], ssem, rsem, device_id=device(to), device_id_type=MESH).start()

def wait_bytes(ref, sem):
    pltpu.make_async_copy(ref, ref, sem).wait()

def rs_sum(pos, geo, s, cur, recv, rsem):
    axes, g, _, (pr, pc), cs = geo[s]
    wait_bytes(recv, rsem)
    r, c = piece(index(pos, axes), cs, pr, pc)
    total = cur[pl.ds(r, pr), pl.ds(c, pc)]
    for n in range(g - 1):
        total = total + recv[n].astype(jnp.float32)
    return total

def regions(pos, geo):
    r0 = c0 = 0
    out = [(0, 0)]
    for axes, g, _, (pr, pc), cs in geo:
        r, c = piece(index(pos, axes), cs, pr, pc)
        r0, c0 = r0 + r, c0 + c
        out.append((pl.multiple_of(r0, 16), pl.multiple_of(c0, 128)))
    return out

def ag_send(pos, geo, regs, s, out, ssem, rsem):
    axes, g, _, (pr, pc), cs = geo[s]
    r, c = regs[s + 1]
    view = out.at[pl.ds(r, pr), pl.ds(c, pc)]
    for n, d in enumerate(offsets(axes)):
        to = partner(pos, axes, d)
        pltpu.make_async_remote_copy(view, view, ssem, rsem, device_id=device(to), device_id_type=MESH).start()


F32, BF16 = jnp.float32, jnp.bfloat16
OUT_ORDER = (2, 1, 3, 0)
IN_ORDER = (2, 1, 3, 0)
TAIL = (
    "s", "e0", "m", "d1", "e1", "d2", "e2", "A0", "A1", "d3", "e3", "B0", "B1", "R0",
    "e4", "d4", "e5", "d5", "g",
)
BLOCKS = [(o, dc) for o in range(3) for dc in range(2)]
ROWS = 32 * len(BLOCKS)
PLANS = [
    ("c", "z", "xy"), ("c", "x", "zy"), ("c", "z", "xy"),
    ("c", "y", "xz"), ("c", "x", "zy"), ("c", "z", "xy"),
]
GEO = [geometry(plan) for plan in PLANS]
FACTOR = float(NB * NP * 3 * NP * 32) ** (-0.5)
STAGES = 3
DEC, ENC = 0, 3


def dot(left, right):
    return jnp.dot(left, right, preferred_element_type=F32)


def dot_back(left, weight):
    return lax.dot_general(left, weight, (((1,), (1,)), ((), ())), preferred_element_type=F32)


def outer(left, right):
    return lax.dot_general(left, right, (((0,), (0,)), ((), ())), preferred_element_type=F32)


def split(value):
    high = value.astype(BF16)
    return high, (value - high.astype(F32)).astype(BF16)


def sigmoid(value):
    return 1.0 / (1.0 + jnp.exp(-value))


def chunk(dy):
    return pl.ds(dy * ROWS, ROWS)


def patch_at(pos, sign, dy, dc):
    return lax.rem(pos["y"] + sign * dy + 4, 4) * 2 + lax.rem(pos["c"] + dc, 2)


def live_only(ref, count, o):
    columns = jnp.transpose(ref[0, o])
    slot = lax.broadcasted_iota(jnp.int32, (32, NP), 0)
    return jnp.transpose(jnp.where(slot < count[o], columns, -1))


def pick(row_of, pos, sign, dy, rows):
    lines = [row_of(o, patch_at(pos, sign, dy, dc)) for o, dc in BLOCKS]
    columns = jnp.transpose(jnp.concatenate(lines + lines[:2], axis=0))
    node = lax.broadcasted_iota(jnp.int32, (32, rows), 1)
    parts = []
    for n in range(len(BLOCKS)):
        parts.append(jnp.where(node == columns[:, n : n + 1], 1.0, 0.0).astype(BF16))
    return jnp.concatenate(parts, axis=0)


def edge_send(sign, dy, b, pos, send, recv, send_sem, recv_sem, cores=(0, 1)):
    for n, (o, dc) in enumerate(BLOCKS):
        if dc not in cores:
            continue
        band = lax.rem(b + sign * (o - 1) + NB, NB)
        src = send.at[dy, pl.ds(n * 32, 32)]
        dst = recv.at[dy, pl.ds(n * 32, 32)]
        if (o, dy, dc) == (1, 0, 0):
            pltpu.make_async_copy(src, dst, recv_sem.at[dy]).start()
        else:
            pltpu.make_async_remote_copy(
                src, dst, send_sem.at[dy], recv_sem.at[dy],
                device_id=(band, patch_at(pos, sign, dy, dc)), device_id_type=MESH,
            ).start()


def greet(b, p, pos):
    bar = pltpu.get_barrier_semaphore()
    n = 0
    for dy in OUT_ORDER:
        for o, dc in BLOCKS:
            if (o, dy, dc) != (1, 0, 0):
                band = lax.rem(b + o - 1 + NB, NB)
                pl.semaphore_signal(
                    bar, inc=1, device_id=(band, patch_at(pos, 1, dy, dc)), device_id_type=MESH
                )
                n += 1
    seen = []
    for plan in PLANS:
        for axes in plan:
            for d in offsets(axes):
                full = tuple(dict(zip(axes, d)).get(a, 0) for a in "zxyc")
                if full not in seen:
                    seen.append(full)
    for d in seen:
        pl.semaphore_signal(
            bar, inc=1, device_id=device(partner(pos, "zxyc", d)), device_id_type=MESH
        )
    return bar, n + len(seen)


class Sum:
    def __init__(self, pos, t, acc, sbf, scr, out, ssem, rsem):
        self.pos, self.geo = pos, GEO[t]
        self.acc, self.sbf, self.out = acc.at[t], sbf.at[t], out.at[t]
        self.scr, self.t = scr[t], t
        self.ssem, self.rsem = ssem, rsem
        self.sibling = partner(pos, "c", (1,))
        self.axis = PLANS[t][1]
        self.half = pos["c"] * 256

    def begin(self):
        other = pl.ds(pl.multiple_of((1 - self.pos["c"]) * 256, 256), 256)
        self.sbf[other, :] = self.acc[other, :].astype(BF16)
        rs_send(self.pos, self.geo, 0, self.sbf, self.scr[0][2],
                self.ssem.at[self.t, 0], self.rsem.at[self.t, 0])

    def reduce(self, s):
        pos, geo, scr, t = self.pos, self.geo, self.scr, self.t
        cur = self.acc if s == 0 else scr[s - 1][0]
        total = rs_sum(pos, geo, s, cur, scr[s][2], self.rsem.at[t, s])
        if s < 2:
            scr[s][0][...] = total
            scr[s][1][...] = total.astype(BF16)
            rs_send(pos, geo, s + 1, scr[s][1], scr[s + 1][2],
                    self.ssem.at[t, s + 1], self.rsem.at[t, s + 1])
        else:
            pr, pc = geo[s][3]
            regs = regions(pos, geo)
            r, c = regs[-1]
            self.out[pl.ds(r, pr), pl.ds(c, pc)] = total.astype(BF16)
            ag_send(pos, geo, regs, 2, self.out, self.ssem.at[t, 4], self.rsem.at[t, 4])

    def rows(self, k):
        place = lax.rem(self.pos[self.axis] - k + 4, 4)
        return self.out.at[pl.ds(pl.multiple_of(self.half + place * 64, 64), 64), :]

    def pass_on(self, k):
        view = self.rows(k)
        pltpu.make_async_remote_copy(
            view, view, self.ssem.at[self.t, 3], self.rsem.at[self.t, 3],
            device_id=device(self.sibling), device_id_type=MESH,
        ).start()

    def gather_plane(self):
        t = self.t
        wait_bytes(self.scr[2][2], self.rsem.at[t, 4])
        view = self.rows(0)
        for d in (2, 1, 3):
            to = partner(self.pos, self.axis, (d,))
            pltpu.make_async_remote_copy(
                view, view, self.ssem.at[t, 5], self.rsem.at[t, 4 + d],
                device_id=device(to), device_id_type=MESH,
            ).start()
        self.pass_on(0)

    def gather_axis(self, d):
        wait_bytes(self.rows(d), self.rsem.at[self.t, 4 + d])
        self.pass_on(d)

    def gather_pair(self):
        wait_bytes(self.scr[0][2], self.rsem.at[self.t, 3])

    def end(self):
        t, scr = self.t, self.scr
        for place, ref in enumerate((scr[0], scr[1], scr[2], scr[0], scr[2], scr[1])):
            wait_bytes(ref[2], self.ssem.at[t, place])


def kernel(
    grid_in, mesh_in, cot_in, es_in, er_in, eo_in, ds_in, dr_in, do_in,
    es_i, er_i, n_e_in, ds_i, dr_i, n_d_in,
    grid_res, mesh_res, o0, o1, o2, o3, o4, o5,
    grid, i_es, i_er, n_e, i_ds, i_dr, n_d, mesh, cot, w_es, w_er, w_eo, w_ds, w_dr, w_do, grid_out, mesh_out, out,
    isem, osem, live, send, recv, oh_es, oh_er, oh_ds, oh_dr, t_es, t_er, t_ds, t_dr,
    enc_pre, dec_pre, dec_back, enc_d, dec_d, acc, sbf, *rest,
):
    scr = []
    for t in range(6):
        n = 9 * t
        scr.append([rest[n + 3 * s : n + 3 * s + 3] for s in range(STAGES)])
    esend, erecv, ssem, rsem = rest[54:]
    results = [o3, o4, o5, o0, o1, o2]
    loads = {}
    for n, (name, src, dst) in enumerate((
        ("i_es", es_i, i_es), ("grid", grid_in, grid), ("i_er", er_i, i_er), ("n_e", n_e_in, n_e),
        ("i_ds", ds_i, i_ds), ("i_dr", dr_i, i_dr), ("n_d", n_d_in, n_d), ("er", er_in, w_er), ("mesh", mesh_in, mesh), ("dr", dr_in, w_dr), ("cot", cot_in, cot),
        ("do", do_in, w_do), ("es", es_in, w_es), ("eo", eo_in, w_eo), ("ds", ds_in, w_ds),
    )):
        loads[name] = pltpu.make_async_copy(src, dst, isem.at[n])
        loads[name].start()

    def store(n, src, dst):
        copy = pltpu.make_async_copy(src, dst, osem.at[n])
        copy.start()
        return copy

    b, p = lax.axis_index("band"), lax.axis_index("patch")
    pos = position()
    bar, greeted = greet(b, p, pos)

    def edges(phase, sign, dy, cores=(0, 1)):
        edge_send(sign, dy, b, pos, send.at[phase], recv.at[phase],
                  esend.at[phase], erecv.at[phase], cores)

    def arrive(phase, o):
        wait_bytes(recv.at[phase, o], erecv.at[phase, o])

    sums = [Sum(pos, t, acc, sbf, scr, out, ssem, rsem) for t in range(6)]
    dec_sums, enc_sums = sums[:3], sums[3:]

    loads["i_es"].wait()
    loads["grid"].wait()
    for n, dy in enumerate(OUT_ORDER):
        oh_es[chunk(dy), :] = pick(lambda o, q: i_es[0, o, pl.ds(q, 1), :], pos, 1, dy, 256)
        send[0, dy] = dot(oh_es[chunk(dy), :], grid[...]).astype(BF16)
        if n == 0:
            pl.semaphore_wait(bar, greeted)
        edges(0, 1, dy)

    for name in ("i_er", "n_e", "i_ds", "i_dr", "n_d"):
        loads[name].wait()
    for o in range(3):
        live[0, o] = live_only(i_er, n_e, o)
        live[1, o] = live_only(i_dr, n_d, o)
    for dy in range(4):
        oh_er[chunk(dy), :] = pick(lambda o, q: live[0, o, pl.ds(q, 1), :], pos, -1, dy, 128)
    t_er[...] = jnp.transpose(oh_er[...])
    loads["er"].wait()
    loads["mesh"].wait()
    high, low = split(dot(mesh[...], w_er[...]))
    for dy in range(4):
        enc_pre[chunk(dy), :] = dot(oh_er[chunk(dy), :], high) + dot(oh_er[chunk(dy), :], low)
    for dy in range(4):
        oh_ds[chunk(dy), :] = pick(lambda o, q: i_ds[0, o, pl.ds(q, 1), :], pos, 1, dy, 128)
        oh_dr[chunk(dy), :] = pick(lambda o, q: live[1, o, pl.ds(q, 1), :], pos, -1, dy, 256)
    t_ds[...] = jnp.transpose(oh_ds[...])
    t_dr[...] = jnp.transpose(oh_dr[...])
    t_es[...] = jnp.transpose(oh_es[...])
    loads["dr"].wait()
    high, low = split(dot(grid[...], w_dr[...]))
    for dy in range(4):
        dec_pre[chunk(dy), :] = dot(oh_dr[chunk(dy), :], high) + dot(oh_dr[chunk(dy), :], low)
    loads["cot"].wait()
    loads["do"].wait()
    high, low = split(dot_back(cot[...], w_do[...]))
    for dy in range(4):
        dec_back[chunk(dy), :] = dot(oh_dr[chunk(dy), :], high) + dot(oh_dr[chunk(dy), :], low)

    for name in ("es", "eo", "ds"):
        loads[name].wait()
    for dy in IN_ORDER:
        arrive(0, dy)
        pre = dot(recv[0, dy], w_es[...]) + enc_pre[chunk(dy), :]
        enc_pre[chunk(dy), :] = pre
        enc_d[chunk(dy), :] = (pre * sigmoid(pre)).astype(BF16)
    high, low = split(dot(t_er[...], enc_d[...]))
    mesh_new = (mesh[...].astype(F32) + (dot(high, w_eo[...]) + dot(low, w_eo[...]))).astype(BF16)
    enc_act_sum = high

    for dy in OUT_ORDER:
        send[1, dy] = dot(oh_ds[chunk(dy), :], mesh_new).astype(BF16)
        edges(1, 1, dy)
    for dy in range(4):
        pre = enc_pre[chunk(dy), :]
        sigma = sigmoid(pre)
        enc_pre[chunk(dy), :] = sigma * (1.0 + pre * (1.0 - sigma))

    for dy in IN_ORDER:
        arrive(1, dy)
        pre = dot(recv[1, dy], w_ds[...]) + dec_pre[chunk(dy), :]
        sigma = sigmoid(pre)
        slope = sigma * (1.0 + pre * (1.0 - sigma))
        dpre = (dec_back[chunk(dy), :] * slope).astype(BF16)
        dec_d[chunk(dy), :] = dpre
        send[2, dy] = dot_back(dpre, w_ds[...]).astype(BF16)
        edges(2, -1, dy)
        enc_d[chunk(dy), :] = (pre * sigma).astype(BF16)

    acc[DEC + 0] = outer(recv[1].reshape(768, 512), dec_d[...])
    dec_sums[0].begin()
    grid_sum = dot(t_dr[...], dec_d[...]).astype(BF16)
    acc[DEC + 1] = outer(grid[...], grid_sum)
    dec_sums[1].begin()
    acc[DEC + 2] = outer(dot(t_dr[...], enc_d[...]).astype(BF16), cot[...])
    dec_sums[2].begin()
    grid_out[...] = cot[...].astype(F32) + dot_back(grid_sum, w_dr[...])
    for one in dec_sums:
        one.reduce(0)
    for dy in IN_ORDER:
        arrive(2, dy)
    mesh_back = dot(t_ds[...], recv[2].reshape(768, 512))
    gmsg = mesh_back.astype(BF16)
    acc[ENC + 2] = outer(enc_act_sum, gmsg)
    enc_sums[2].begin()
    high, low = split(dot_back(gmsg, w_eo[...]))
    for dy in range(4):
        back = dot(oh_er[chunk(dy), :], high) + dot(oh_er[chunk(dy), :], low)
        enc_d[chunk(dy), :] = (back * enc_pre[chunk(dy), :]).astype(BF16)
    acc[ENC + 0] = outer(recv[0].reshape(768, 512), enc_d[...])
    enc_sums[0].begin()
    mesh_sum = dot(t_er[...], enc_d[...]).astype(BF16)
    acc[ENC + 1] = outer(mesh[...], mesh_sum)
    enc_sums[1].begin()

    stores = []

    def advance(group, n):
        if n == 4:
            for d in (1, 3, 2):
                for one in group:
                    one.gather_axis(d)
            return
        for one in group:
            if n < 3:
                one.reduce(n)
            elif n == 3:
                one.gather_plane()
            else:
                one.gather_pair()
                stores.append(store(one.t, one.out, results[one.t]))

    for token in TAIL:
        if token[0] == "d":
            advance(dec_sums, int(token[1]))
        elif token[0] == "e":
            advance((enc_sums[2], enc_sums[0], enc_sums[1]), int(token[1]))
        elif token[0] in "RAB":
            for dy in {"R": (0,), "A": (2,), "B": (1, 3)}[token[0]]:
                edges(3, -1, dy, (0, 1) if token[0] == "R" else (int(token[1]),))
        elif token == "s":
            for dy in OUT_ORDER:
                send[3, dy] = dot_back(enc_d[chunk(dy), :], w_es[...]).astype(BF16)
        elif token == "m":
            mesh_out[...] = mesh_back + dot_back(mesh_sum, w_er[...])
            stores.append(store(6, mesh_out, mesh_res))
        elif token == "g":
            for dy in OUT_ORDER:
                arrive(3, dy)
            grid_out[...] = grid_out[...] + dot(t_es[...], recv[3].reshape(768, 512))
            stores.append(store(7, grid_out, grid_res))

    for phase in range(4):
        for dy in range(4):
            sent = send.at[phase, dy] if dy else send.at[phase, dy, pl.ds(0, ROWS - 32)]
            wait_bytes(sent, esend.at[phase, dy])
    for one in sums:
        one.end()
    for one in stores:
        one.wait()


def finish(grid_in, mesh_in, *refs):
    sums, (grid_out, mesh_out), outs = refs[:6], refs[6:8], refs[8:14]
    narrow, wide, grid_rows, mesh_rows, in_sem, out_sem = refs[14:]
    loads = [pltpu.make_async_copy(sums[t], narrow.at[t], in_sem.at[t]) for t in range(6)]
    stores = [pltpu.make_async_copy(wide.at[t], outs[t], out_sem.at[t]) for t in range(6)]
    loads.append(pltpu.make_async_copy(grid_in, grid_rows, in_sem.at[6]))
    loads.append(pltpu.make_async_copy(mesh_in, mesh_rows, in_sem.at[7]))
    stores.append(pltpu.make_async_copy(grid_rows, grid_out, out_sem.at[6]))
    stores.append(pltpu.make_async_copy(mesh_rows, mesh_out, out_sem.at[7]))
    for n in (6, 0, 1, 2, 3, 4, 5, 7):
        loads[n].start()
    for n in (6, 7):
        loads[n].wait()
        stores[n].start()
    for t in range(6):
        loads[t].wait()
        wide[t] = narrow[t].astype(F32) * FACTOR
        stores[t].start()
    for one in stores:
        one.wait()


def per_device(
    grid_latent, mesh_latent, grid_cotangent,
    enc_w_send, enc_w_recv, enc_w_out, dec_w_send, dec_w_recv, dec_w_out,
    enc_sender, enc_receiver, enc_count, dec_sender, dec_receiver, dec_count,
):
    anywhere = pl.BlockSpec(memory_space=pl.ANY)
    weight = pltpu.VMEM((512, 512), BF16)
    index = pltpu.VMEM((1, 3, NP, 32), jnp.int32)
    count = pltpu.VMEM((3, 1, NP), jnp.int32)
    scratch = [
        pltpu.VMEM((256, 512), BF16),
        index, index, count, index, index, count,
        pltpu.VMEM((128, 512), BF16),
        pltpu.VMEM((256, 512), BF16),
    ] + [weight] * 6 + [
        pltpu.VMEM((256, 512), F32),
        pltpu.VMEM((128, 512), F32),
        pltpu.VMEM((6, 512, 512), BF16),
        pltpu.SemaphoreType.DMA((15,)),
        pltpu.SemaphoreType.DMA((8,)),
        pltpu.VMEM((2, 3, NP, 32), jnp.int32),
        pltpu.VMEM((4, 4, ROWS, 512), BF16),
        pltpu.VMEM((4, 4, ROWS, 512), BF16),
        pltpu.VMEM((768, 256), BF16),
        pltpu.VMEM((768, 128), BF16),
        pltpu.VMEM((768, 128), BF16),
        pltpu.VMEM((768, 256), BF16),
        pltpu.VMEM((256, 768), BF16),
        pltpu.VMEM((128, 768), BF16),
        pltpu.VMEM((128, 768), BF16),
        pltpu.VMEM((256, 768), BF16),
        pltpu.VMEM((768, 512), F32),
        pltpu.VMEM((768, 512), F32),
        pltpu.VMEM((768, 512), F32),
        pltpu.VMEM((768, 512), BF16),
        pltpu.VMEM((768, 512), BF16),
        pltpu.VMEM((6, 512, 512), F32),
        pltpu.VMEM((6, 512, 512), BF16),
    ]
    for t in range(6):
        scratch += scratch_for(PLANS[t])
    scratch += [pltpu.SemaphoreType.DMA((4, 4))] * 2
    scratch += [pltpu.SemaphoreType.DMA((6, 6)), pltpu.SemaphoreType.DMA((6, 8))]
    square = jax.ShapeDtypeStruct((512, 512), BF16)
    rows = [jax.ShapeDtypeStruct((256, 512), F32), jax.ShapeDtypeStruct((128, 512), F32)]
    results = pl.pallas_call(
        kernel,
        out_shape=rows + [square] * 6,
        in_specs=[anywhere] * 15,
        out_specs=[anywhere] * 8,
        scratch_shapes=scratch,
        compiler_params=pltpu.CompilerParams(
            collective_id=0, has_side_effects=True, vmem_limit_bytes=56 << 20
        ),
    )(
        grid_latent, mesh_latent, grid_cotangent,
        enc_w_send, enc_w_recv, enc_w_out, dec_w_send, dec_w_recv, dec_w_out,
        enc_sender, enc_receiver, jnp.transpose(enc_count, (1, 0, 2)),
        dec_sender, dec_receiver, jnp.transpose(dec_count, (1, 0, 2)),
    )
    return pl.pallas_call(
        finish,
        out_shape=rows + [jax.ShapeDtypeStruct((512, 512), F32)] * 6,
        in_specs=[anywhere] * 8,
        out_specs=[anywhere] * 8,
        scratch_shapes=[
            pltpu.VMEM((6, 512, 512), BF16),
            pltpu.VMEM((6, 512, 512), F32),
            pltpu.VMEM((256, 512), F32),
            pltpu.VMEM((128, 512), F32),
            pltpu.SemaphoreType.DMA((8,)),
            pltpu.SemaphoreType.DMA((8,)),
        ],
        compiler_params=pltpu.CompilerParams(vmem_limit_bytes=60 << 20),
    )(*results)


def solution(mesh):
    in_specs = (
        P(("band", "patch"), None),
        P(("band", "patch"), None),
        P(("band", "patch"), None),
        P(),
        P(),
        P(),
        P(),
        P(),
        P(),
        P(("band", "patch"), None, None, None),
        P(("band", "patch"), None, None, None),
        P(("band", "patch"), None, None),
        P(("band", "patch"), None, None, None),
        P(("band", "patch"), None, None, None),
        P(("band", "patch"), None, None),
    )
    out_specs = (
        P(("band", "patch"), None),
        P(("band", "patch"), None),
        P(),
        P(),
        P(),
        P(),
        P(),
        P(),
    )
    return jax.shard_map(
        per_device, mesh=mesh, in_specs=in_specs, out_specs=out_specs, check_vma=False
    )
```

```python
import functools
import itertools

import jax
import jax.numpy as jnp
from jax import lax
from jax.experimental import pallas as pl
from jax.experimental.pallas import tpu as pltpu
from jax.sharding import PartitionSpec as P


MESH = pl.DeviceIdType.MESH
NB, NP = 16, 8
SIZES = {"z": 4, "x": 4, "y": 4, "c": 2}

def position():
    b, p = lax.axis_index("band"), lax.axis_index("patch")
    return {"z": b // 4, "x": lax.rem(b, 4), "y": p // 2, "c": lax.rem(p, 2)}

def device(pos):
    return (pos["z"] * 4 + pos["x"], pos["y"] * 2 + pos["c"])

def offsets(axes):
    return [d for d in itertools.product(*[range(SIZES[a]) for a in axes]) if any(d)]

def partner(pos, axes, d):
    new = dict(pos)
    for a, k in zip(axes, d):
        new[a] = lax.rem(pos[a] + k, SIZES[a])
    return new

def index(pos, axes):
    i = 0
    for a in axes:
        i = i * SIZES[a] + pos[a]
    return i

def geometry(plan):
    R = C = 512
    out = []
    for axes in plan:
        g = 1
        for a in axes:
            g *= SIZES[a]
        rs = min(g, R // 16)
        cs = g // rs
        out.append((axes, g, (R, C), (R // rs, C // cs), cs))
        R, C = R // rs, C // cs
    return out

def scratch_for(plan):
    shapes = []
    for axes, g, (R, C), (pr, pc), cs in geometry(plan):
        shapes += [pltpu.VMEM((pr, pc), jnp.float32), pltpu.VMEM((pr, pc), jnp.bfloat16), pltpu.VMEM((g - 1, pr, pc), jnp.bfloat16)]
    return shapes

def piece(k, cs, pr, pc):
    r = (k // cs) * pr
    c = lax.rem(k, cs) * pc if cs > 1 else 0
    r = pl.multiple_of(r, 16) if not isinstance(r, int) else r
    if cs > 1: c = pl.multiple_of(c, 128)
    return r, c

def rs_send(pos, geo, s, srcb, recv, ssem, rsem):
    axes, g, _, (pr, pc), cs = geo[s]
    for n, d in enumerate(offsets(axes)):
        to = partner(pos, axes, d)
        r, c = piece(index(to, axes), cs, pr, pc)
        pltpu.make_async_remote_copy(srcb.at[pl.ds(r, pr), pl.ds(c, pc)], recv.at[n], ssem, rsem, device_id=device(to), device_id_type=MESH).start()

def wait_bytes(ref, sem):
    pltpu.make_async_copy(ref, ref, sem).wait()

def rs_sum(pos, geo, s, cur, recv, rsem):
    axes, g, _, (pr, pc), cs = geo[s]
    wait_bytes(recv, rsem)
    r, c = piece(index(pos, axes), cs, pr, pc)
    total = cur[pl.ds(r, pr), pl.ds(c, pc)]
    for n in range(g - 1):
        total = total + recv[n].astype(jnp.float32)
    return total

def regions(pos, geo):
    r0 = c0 = 0
    out = [(0, 0)]
    for axes, g, _, (pr, pc), cs in geo:
        r, c = piece(index(pos, axes), cs, pr, pc)
        r0, c0 = r0 + r, c0 + c
        out.append((pl.multiple_of(r0, 16), pl.multiple_of(c0, 128)))
    return out

def ag_send(pos, geo, regs, s, out, ssem, rsem):
    axes, g, _, (pr, pc), cs = geo[s]
    r, c = regs[s + 1]
    view = out.at[pl.ds(r, pr), pl.ds(c, pc)]
    for n, d in enumerate(offsets(axes)):
        to = partner(pos, axes, d)
        pltpu.make_async_remote_copy(view, view, ssem, rsem, device_id=device(to), device_id_type=MESH).start()


F32, BF16 = jnp.float32, jnp.bfloat16
OUT_ORDER = (2, 1, 3, 0)
IN_ORDER = (2, 1, 3, 0)
TAIL = (
    "s", "e0", "m", "d1", "e1", "d2", "e2", "A0", "A1", "d3", "e3", "B0", "B1", "R0",
    "e4", "d4", "e5", "d5", "g",
)
BLOCKS = [(o, dc) for o in range(3) for dc in range(2)]
ROWS = 32 * len(BLOCKS)
PLANS = [
    ("c", "z", "xy"), ("c", "x", "zy"), ("c", "z", "xy"),
    ("c", "y", "xz"), ("c", "x", "zy"), ("c", "z", "xy"),
]
GEO = [geometry(plan) for plan in PLANS]
FACTOR = float(NB * NP * 3 * NP * 32) ** (-0.5)
STAGES = 3
DEC, ENC = 0, 3


def dot(left, right):
    return jnp.dot(left, right, preferred_element_type=F32)


def dot_back(left, weight):
    return lax.dot_general(left, weight, (((1,), (1,)), ((), ())), preferred_element_type=F32)


def outer(left, right):
    return lax.dot_general(left, right, (((0,), (0,)), ((), ())), preferred_element_type=F32)


def split(value):
    high = value.astype(BF16)
    return high, (value - high.astype(F32)).astype(BF16)


def sigmoid(value):
    return 1.0 / (1.0 + jnp.exp(-value))


def chunk(dy):
    return pl.ds(dy * ROWS, ROWS)


def patch_at(pos, sign, dy, dc):
    return lax.rem(pos["y"] + sign * dy + 4, 4) * 2 + lax.rem(pos["c"] + dc, 2)


def live_only(ref, count, o):
    columns = jnp.transpose(ref[0, o])
    slot = lax.broadcasted_iota(jnp.int32, (32, NP), 0)
    return jnp.transpose(jnp.where(slot < count[o], columns, -1))


def pick(row_of, pos, sign, dy, rows):
    lines = [row_of(o, patch_at(pos, sign, dy, dc)) for o, dc in BLOCKS]
    columns = jnp.transpose(jnp.concatenate(lines + lines[:2], axis=0))
    node = lax.broadcasted_iota(jnp.int32, (32, rows), 1)
    parts = []
    for n in range(len(BLOCKS)):
        parts.append(jnp.where(node == columns[:, n : n + 1], 1.0, 0.0).astype(BF16))
    return jnp.concatenate(parts, axis=0)


def edge_send(sign, dy, b, pos, send, recv, send_sem, recv_sem, cores=(0, 1)):
    for n, (o, dc) in enumerate(BLOCKS):
        if dc not in cores:
            continue
        band = lax.rem(b + sign * (o - 1) + NB, NB)
        src = send.at[dy, pl.ds(n * 32, 32)]
        dst = recv.at[dy, pl.ds(n * 32, 32)]
        if (o, dy, dc) == (1, 0, 0):
            pltpu.make_async_copy(src, dst, recv_sem.at[dy]).start()
        else:
            pltpu.make_async_remote_copy(
                src, dst, send_sem.at[dy], recv_sem.at[dy],
                device_id=(band, patch_at(pos, sign, dy, dc)), device_id_type=MESH,
            ).start()


def greet(b, p, pos):
    bar = pltpu.get_barrier_semaphore()
    n = 0
    for dy in OUT_ORDER:
        for o, dc in BLOCKS:
            if (o, dy, dc) != (1, 0, 0):
                band = lax.rem(b + o - 1 + NB, NB)
                pl.semaphore_signal(
                    bar, inc=1, device_id=(band, patch_at(pos, 1, dy, dc)), device_id_type=MESH
                )
                n += 1
    seen = []
    for plan in PLANS:
        for axes in plan:
            for d in offsets(axes):
                full = tuple(dict(zip(axes, d)).get(a, 0) for a in "zxyc")
                if full not in seen:
                    seen.append(full)
    for d in seen:
        pl.semaphore_signal(
            bar, inc=1, device_id=device(partner(pos, "zxyc", d)), device_id_type=MESH
        )
    return bar, n + len(seen)


class Sum:
    def __init__(self, pos, t, acc, sbf, scr, out, ssem, rsem):
        self.pos, self.geo = pos, GEO[t]
        self.acc, self.sbf, self.out = acc.at[t], sbf.at[t], out.at[t]
        self.scr, self.t = scr[t], t
        self.ssem, self.rsem = ssem, rsem
        self.sibling = partner(pos, "c", (1,))
        self.axis = PLANS[t][1]
        self.half = pos["c"] * 256

    def begin(self):
        other = pl.ds(pl.multiple_of((1 - self.pos["c"]) * 256, 256), 256)
        self.sbf[other, :] = self.acc[other, :].astype(BF16)
        rs_send(self.pos, self.geo, 0, self.sbf, self.scr[0][2],
                self.ssem.at[self.t, 0], self.rsem.at[self.t, 0])

    def reduce(self, s):
        pos, geo, scr, t = self.pos, self.geo, self.scr, self.t
        cur = self.acc if s == 0 else scr[s - 1][0]
        total = rs_sum(pos, geo, s, cur, scr[s][2], self.rsem.at[t, s])
        if s < 2:
            scr[s][0][...] = total
            scr[s][1][...] = total.astype(BF16)
            rs_send(pos, geo, s + 1, scr[s][1], scr[s + 1][2],
                    self.ssem.at[t, s + 1], self.rsem.at[t, s + 1])
        else:
            pr, pc = geo[s][3]
            regs = regions(pos, geo)
            r, c = regs[-1]
            self.out[pl.ds(r, pr), pl.ds(c, pc)] = total.astype(BF16)
            ag_send(pos, geo, regs, 2, self.out, self.ssem.at[t, 4], self.rsem.at[t, 4])

    def rows(self, k):
        place = lax.rem(self.pos[self.axis] - k + 4, 4)
        return self.out.at[pl.ds(pl.multiple_of(self.half + place * 64, 64), 64), :]

    def pass_on(self, k):
        view = self.rows(k)
        pltpu.make_async_remote_copy(
            view, view, self.ssem.at[self.t, 3], self.rsem.at[self.t, 3],
            device_id=device(self.sibling), device_id_type=MESH,
        ).start()

    def gather_plane(self):
        t = self.t
        wait_bytes(self.scr[2][2], self.rsem.at[t, 4])
        view = self.rows(0)
        for d in (2, 1, 3):
            to = partner(self.pos, self.axis, (d,))
            pltpu.make_async_remote_copy(
                view, view, self.ssem.at[t, 5], self.rsem.at[t, 4 + d],
                device_id=device(to), device_id_type=MESH,
            ).start()
        self.pass_on(0)

    def gather_axis(self, d):
        wait_bytes(self.rows(d), self.rsem.at[self.t, 4 + d])
        self.pass_on(d)

    def gather_pair(self):
        wait_bytes(self.scr[0][2], self.rsem.at[self.t, 3])

    def end(self):
        t, scr = self.t, self.scr
        for place, ref in enumerate((scr[0], scr[1], scr[2], scr[0], scr[2], scr[1])):
            wait_bytes(ref[2], self.ssem.at[t, place])


def kernel(
    grid_in, mesh_in, cot_in, es_in, er_in, eo_in, ds_in, dr_in, do_in,
    es_i, er_i, n_e_in, ds_i, dr_i, n_d_in,
    grid_res, mesh_res, o0, o1, o2, o3, o4, o5,
    grid, i_es, i_er, n_e, i_ds, i_dr, n_d, mesh, cot, w_es, w_er, w_eo, w_ds, w_dr, w_do, grid_out, mesh_out, out,
    isem, osem, live, t_rows, t_mesh, t_act, send, recv, oh_es, oh_er, oh_ds, oh_dr, t_es, t_er, t_ds, t_dr,
    enc_pre, dec_pre, dec_back, enc_d, dec_d, acc, sbf, *rest,
):
    scr = []
    for t in range(6):
        n = 9 * t
        scr.append([rest[n + 3 * s : n + 3 * s + 3] for s in range(STAGES)])
    esend, erecv, ssem, rsem = rest[54:]
    results = [o3, o4, o5, o0, o1, o2]
    loads = {}
    for n, (name, src, dst) in enumerate((
        ("i_es", es_i, i_es), ("grid", grid_in, grid), ("i_er", er_i, i_er), ("n_e", n_e_in, n_e),
        ("i_ds", ds_i, i_ds), ("i_dr", dr_i, i_dr), ("n_d", n_d_in, n_d), ("er", er_in, w_er), ("mesh", mesh_in, mesh), ("dr", dr_in, w_dr), ("cot", cot_in, cot),
        ("do", do_in, w_do), ("es", es_in, w_es), ("eo", eo_in, w_eo), ("ds", ds_in, w_ds),
    )):
        loads[name] = pltpu.make_async_copy(src, dst, isem.at[n])
        loads[name].start()

    def store(n, src, dst):
        copy = pltpu.make_async_copy(src, dst, osem.at[n])
        copy.start()
        return copy

    b, p = lax.axis_index("band"), lax.axis_index("patch")
    pos = position()
    bar, greeted = greet(b, p, pos)

    def edges(phase, sign, dy, cores=(0, 1)):
        edge_send(sign, dy, b, pos, send.at[phase], recv.at[phase],
                  esend.at[phase], erecv.at[phase], cores)

    def arrive(phase, o):
        wait_bytes(recv.at[phase, o], erecv.at[phase, o])

    sums = [Sum(pos, t, acc, sbf, scr, out, ssem, rsem) for t in range(6)]
    dec_sums, enc_sums = sums[:3], sums[3:]

    loads["i_es"].wait()
    loads["grid"].wait()
    for n, dy in enumerate(OUT_ORDER):
        oh_es[chunk(dy), :] = pick(lambda o, q: i_es[0, o, pl.ds(q, 1), :], pos, 1, dy, 256)
        send[0, dy] = dot(oh_es[chunk(dy), :], grid[...]).astype(BF16)
        if n == 0:
            pl.semaphore_wait(bar, greeted)
        edges(0, 1, dy)

    for name in ("i_er", "n_e", "i_ds", "i_dr", "n_d"):
        loads[name].wait()
    for o in range(3):
        live[0, o] = live_only(i_er, n_e, o)
        live[1, o] = live_only(i_dr, n_d, o)
    for dy in range(4):
        oh_er[chunk(dy), :] = pick(lambda o, q: live[0, o, pl.ds(q, 1), :], pos, -1, dy, 128)
    t_er[...] = jnp.transpose(oh_er[...])
    loads["er"].wait()
    loads["mesh"].wait()
    high, low = split(dot(mesh[...], w_er[...]))
    for dy in range(4):
        enc_pre[chunk(dy), :] = dot(oh_er[chunk(dy), :], high) + dot(oh_er[chunk(dy), :], low)
    for dy in range(4):
        oh_ds[chunk(dy), :] = pick(lambda o, q: i_ds[0, o, pl.ds(q, 1), :], pos, 1, dy, 128)
        oh_dr[chunk(dy), :] = pick(lambda o, q: live[1, o, pl.ds(q, 1), :], pos, -1, dy, 256)
    t_ds[...] = jnp.transpose(oh_ds[...])
    t_dr[...] = jnp.transpose(oh_dr[...])
    t_es[...] = jnp.transpose(oh_es[...])
    loads["dr"].wait()
    high, low = split(dot(grid[...], w_dr[...]))
    for dy in range(4):
        dec_pre[chunk(dy), :] = dot(oh_dr[chunk(dy), :], high) + dot(oh_dr[chunk(dy), :], low)
    loads["cot"].wait()
    loads["do"].wait()
    high, low = split(dot_back(cot[...], w_do[...]))
    for dy in range(4):
        dec_back[chunk(dy), :] = dot(oh_dr[chunk(dy), :], high) + dot(oh_dr[chunk(dy), :], low)

    for name in ("es", "eo", "ds"):
        loads[name].wait()
    for dy in IN_ORDER:
        arrive(0, dy)
        pre = dot(recv[0, dy], w_es[...]) + enc_pre[chunk(dy), :]
        enc_pre[chunk(dy), :] = pre
        enc_d[chunk(dy), :] = (pre * sigmoid(pre)).astype(BF16)
    high, low = split(dot(t_er[...], enc_d[...]))
    mesh_new = (mesh[...].astype(F32) + (dot(high, w_eo[...]) + dot(low, w_eo[...]))).astype(BF16)
    enc_act_sum = high

    for dy in OUT_ORDER:
        send[1, dy] = dot(oh_ds[chunk(dy), :], mesh_new).astype(BF16)
        edges(1, 1, dy)
    for dy in range(4):
        pre = enc_pre[chunk(dy), :]
        sigma = sigmoid(pre)
        enc_pre[chunk(dy), :] = sigma * (1.0 + pre * (1.0 - sigma))

    t_rows[...] = jnp.transpose(recv[0].reshape(768, 512))
    t_mesh[...] = jnp.transpose(mesh[...])
    t_act[...] = jnp.transpose(enc_act_sum)

    for dy in IN_ORDER:
        arrive(1, dy)
        pre = dot(recv[1, dy], w_ds[...]) + dec_pre[chunk(dy), :]
        sigma = sigmoid(pre)
        slope = sigma * (1.0 + pre * (1.0 - sigma))
        dpre = (dec_back[chunk(dy), :] * slope).astype(BF16)
        dec_d[chunk(dy), :] = dpre
        send[2, dy] = dot_back(dpre, w_ds[...]).astype(BF16)
        edges(2, -1, dy)
        enc_d[chunk(dy), :] = (pre * sigma).astype(BF16)

    acc[DEC + 0] = outer(recv[1].reshape(768, 512), dec_d[...])
    dec_sums[0].begin()
    grid_sum = dot(t_dr[...], dec_d[...]).astype(BF16)
    acc[DEC + 1] = outer(grid[...], grid_sum)
    dec_sums[1].begin()
    acc[DEC + 2] = outer(dot(t_dr[...], enc_d[...]).astype(BF16), cot[...])
    dec_sums[2].begin()
    grid_out[...] = cot[...].astype(F32) + dot_back(grid_sum, w_dr[...])
    for one in dec_sums:
        one.reduce(0)
    for dy in IN_ORDER:
        arrive(2, dy)
    mesh_back = dot(t_ds[...], recv[2].reshape(768, 512))
    gmsg = mesh_back.astype(BF16)
    acc[ENC + 2] = dot(t_act[...], gmsg)
    enc_sums[2].begin()
    high, low = split(dot_back(gmsg, w_eo[...]))
    for dy in range(4):
        back = dot(oh_er[chunk(dy), :], high) + dot(oh_er[chunk(dy), :], low)
        enc_d[chunk(dy), :] = (back * enc_pre[chunk(dy), :]).astype(BF16)
    acc[ENC + 0] = dot(t_rows[...], enc_d[...])
    enc_sums[0].begin()
    mesh_sum = dot(t_er[...], enc_d[...]).astype(BF16)
    acc[ENC + 1] = dot(t_mesh[...], mesh_sum)
    enc_sums[1].begin()

    stores = []

    def advance(group, n):
        if n == 4:
            for d in (1, 3, 2):
                for one in group:
                    one.gather_axis(d)
            return
        for one in group:
            if n < 3:
                one.reduce(n)
            elif n == 3:
                one.gather_plane()
            else:
                one.gather_pair()
                stores.append(store(one.t, one.out, results[one.t]))

    for token in TAIL:
        if token[0] == "d":
            advance(dec_sums, int(token[1]))
        elif token[0] == "e":
            advance((enc_sums[2], enc_sums[0], enc_sums[1]), int(token[1]))
        elif token[0] in "RAB":
            for dy in {"R": (0,), "A": (2,), "B": (1, 3)}[token[0]]:
                edges(3, -1, dy, (0, 1) if token[0] == "R" else (int(token[1]),))
        elif token == "s":
            for dy in OUT_ORDER:
                send[3, dy] = dot_back(enc_d[chunk(dy), :], w_es[...]).astype(BF16)
        elif token == "m":
            mesh_out[...] = mesh_back + dot_back(mesh_sum, w_er[...])
            stores.append(store(6, mesh_out, mesh_res))
        elif token == "g":
            for dy in OUT_ORDER:
                arrive(3, dy)
            grid_out[...] = grid_out[...] + dot(t_es[...], recv[3].reshape(768, 512))
            stores.append(store(7, grid_out, grid_res))

    for phase in range(4):
        for dy in range(4):
            sent = send.at[phase, dy] if dy else send.at[phase, dy, pl.ds(0, ROWS - 32)]
            wait_bytes(sent, esend.at[phase, dy])
    for one in sums:
        one.end()
    for one in stores:
        one.wait()


def finish(grid_in, mesh_in, *refs):
    sums, (grid_out, mesh_out), outs = refs[:6], refs[6:8], refs[8:14]
    narrow, wide, grid_rows, mesh_rows, in_sem, out_sem = refs[14:]
    loads = [pltpu.make_async_copy(sums[t], narrow.at[t], in_sem.at[t]) for t in range(6)]
    stores = [pltpu.make_async_copy(wide.at[t], outs[t], out_sem.at[t]) for t in range(6)]
    loads.append(pltpu.make_async_copy(grid_in, grid_rows, in_sem.at[6]))
    loads.append(pltpu.make_async_copy(mesh_in, mesh_rows, in_sem.at[7]))
    stores.append(pltpu.make_async_copy(grid_rows, grid_out, out_sem.at[6]))
    stores.append(pltpu.make_async_copy(mesh_rows, mesh_out, out_sem.at[7]))
    for n in (6, 0, 1, 2, 3, 4, 5, 7):
        loads[n].start()
    for n in (6, 7):
        loads[n].wait()
        stores[n].start()
    for t in range(6):
        loads[t].wait()
        wide[t] = narrow[t].astype(F32) * FACTOR
        stores[t].start()
    for one in stores:
        one.wait()


def per_device(
    grid_latent, mesh_latent, grid_cotangent,
    enc_w_send, enc_w_recv, enc_w_out, dec_w_send, dec_w_recv, dec_w_out,
    enc_sender, enc_receiver, enc_count, dec_sender, dec_receiver, dec_count,
):
    anywhere = pl.BlockSpec(memory_space=pl.ANY)
    weight = pltpu.VMEM((512, 512), BF16)
    index = pltpu.VMEM((1, 3, NP, 32), jnp.int32)
    count = pltpu.VMEM((3, 1, NP), jnp.int32)
    scratch = [
        pltpu.VMEM((256, 512), BF16),
        index, index, count, index, index, count,
        pltpu.VMEM((128, 512), BF16),
        pltpu.VMEM((256, 512), BF16),
    ] + [weight] * 6 + [
        pltpu.VMEM((256, 512), F32),
        pltpu.VMEM((128, 512), F32),
        pltpu.VMEM((6, 512, 512), BF16),
        pltpu.SemaphoreType.DMA((15,)),
        pltpu.SemaphoreType.DMA((8,)),
        pltpu.VMEM((2, 3, NP, 32), jnp.int32),
        pltpu.VMEM((512, 768), BF16),
        pltpu.VMEM((512, 128), BF16),
        pltpu.VMEM((512, 128), BF16),
        pltpu.VMEM((4, 4, ROWS, 512), BF16),
        pltpu.VMEM((4, 4, ROWS, 512), BF16),
        pltpu.VMEM((768, 256), BF16),
        pltpu.VMEM((768, 128), BF16),
        pltpu.VMEM((768, 128), BF16),
        pltpu.VMEM((768, 256), BF16),
        pltpu.VMEM((256, 768), BF16),
        pltpu.VMEM((128, 768), BF16),
        pltpu.VMEM((128, 768), BF16),
        pltpu.VMEM((256, 768), BF16),
        pltpu.VMEM((768, 512), F32),
        pltpu.VMEM((768, 512), F32),
        pltpu.VMEM((768, 512), F32),
        pltpu.VMEM((768, 512), BF16),
        pltpu.VMEM((768, 512), BF16),
        pltpu.VMEM((6, 512, 512), F32),
        pltpu.VMEM((6, 512, 512), BF16),
    ]
    for t in range(6):
        scratch += scratch_for(PLANS[t])
    scratch += [pltpu.SemaphoreType.DMA((4, 4))] * 2
    scratch += [pltpu.SemaphoreType.DMA((6, 6)), pltpu.SemaphoreType.DMA((6, 8))]
    square = jax.ShapeDtypeStruct((512, 512), BF16)
    rows = [jax.ShapeDtypeStruct((256, 512), F32), jax.ShapeDtypeStruct((128, 512), F32)]
    results = pl.pallas_call(
        kernel,
        out_shape=rows + [square] * 6,
        in_specs=[anywhere] * 15,
        out_specs=[anywhere] * 8,
        scratch_shapes=scratch,
        compiler_params=pltpu.CompilerParams(
            collective_id=0, has_side_effects=True, vmem_limit_bytes=56 << 20
        ),
    )(
        grid_latent, mesh_latent, grid_cotangent,
        enc_w_send, enc_w_recv, enc_w_out, dec_w_send, dec_w_recv, dec_w_out,
        enc_sender, enc_receiver, jnp.transpose(enc_count, (1, 0, 2)),
        dec_sender, dec_receiver, jnp.transpose(dec_count, (1, 0, 2)),
    )
    return pl.pallas_call(
        finish,
        out_shape=rows + [jax.ShapeDtypeStruct((512, 512), F32)] * 6,
        in_specs=[anywhere] * 8,
        out_specs=[anywhere] * 8,
        scratch_shapes=[
            pltpu.VMEM((6, 512, 512), BF16),
            pltpu.VMEM((6, 512, 512), F32),
            pltpu.VMEM((256, 512), F32),
            pltpu.VMEM((128, 512), F32),
            pltpu.SemaphoreType.DMA((8,)),
            pltpu.SemaphoreType.DMA((8,)),
        ],
        compiler_params=pltpu.CompilerParams(vmem_limit_bytes=60 << 20),
    )(*results)


def solution(mesh):
    in_specs = (
        P(("band", "patch"), None),
        P(("band", "patch"), None),
        P(("band", "patch"), None),
        P(),
        P(),
        P(),
        P(),
        P(),
        P(),
        P(("band", "patch"), None, None, None),
        P(("band", "patch"), None, None, None),
        P(("band", "patch"), None, None),
        P(("band", "patch"), None, None, None),
        P(("band", "patch"), None, None, None),
        P(("band", "patch"), None, None),
    )
    out_specs = (
        P(("band", "patch"), None),
        P(("band", "patch"), None),
        P(),
        P(),
        P(),
        P(),
        P(),
        P(),
    )
    return jax.shard_map(
        per_device, mesh=mesh, in_specs=in_specs, out_specs=out_specs, check_vma=False
    )
```
